512 devices in a mesh: dp: 4 (over z_lo, core), fsdp: 32 (over z_hi, y), seq: 4 (over x).
Axes of the slice: x: 4, y: 8, z: 8 (z_hi: 4, z_lo: 2; z = z_hi * 2 + z_lo), core: 2. Of those that a mesh axis runs over, the one named last changes fastest.
Arguments:
- layer_input: bfloat16 [256, 256, 8192], P(('dp', 'fsdp'), 'seq'), may hold values from -6 to 6
- next_token_rows: bfloat16 [256, 256, 8192], P(('dp', 'fsdp'), 'seq'), may hold values from -0.0625 to 0.0625
- response_length: int32 [256], P(('dp', 'fsdp')), may hold values from 32 to 256, as said below
- input_norm_scale: float32 [8192], replicated, may hold values from 0.1 to 1.9
- query_weight: bfloat16 [8192, 128], P('fsdp'), may hold values from -0.0625 to 0.0625
- key_weight: bfloat16 [8192, 128], P('fsdp'), may hold values from -0.0625 to 0.0625
- value_weight: bfloat16 [8192, 128], P('fsdp'), may hold values from -0.0625 to 0.0625
- output_projection_weight: bfloat16 [8192, 128], P('fsdp'), may hold values from -0.5 to 0.5
- adapter_down_weight: bfloat16 [8192, 64], P('fsdp'), may hold values from -0.0625 to 0.0625
- adapter_up_weight: bfloat16 [64, 128], replicated, may hold values from -0.75 to 0.75
Outputs:
- dpo_loss: float32 [], replicated
- grad_down: float32 [8192, 64], P(('fsdp', 'seq'))
- grad_up: float32 [64, 128], replicated
The draws below stay inside these ranges and needn't reach their ends.
Inputs may be any that keep to these rules, and one draw needn't show every extreme that they name: `response_length`: every draw has a sequence with the longest and one with the shortest response.
All inputs are finite; a program needn't handle non-finite values.
Results may differ from the reference program's by a relative error of at most 0.013.
Values may be sent and summed in bfloat16 or wider, within the bound.
A program may use at most 64 MiB of HBM per device.

```python
import math
import jax
import jax.numpy as jnp
from jax import lax

MODEL_DIM = 8192
HEAD_DIM = 128
ADAPTER_ORDER = 64
LEN = 256
PAIRS = 128
SEQS = 256


def draw_response_length(key, part):
    key = jax.random.fold_in(key, 7)
    drawn = jax.random.randint(key, (SEQS,), LEN // 8, LEN + 1)
    drawn = drawn.at[0].set(LEN)
    return drawn.at[SEQS - 1].set(LEN // 8).astype(jnp.int32)


def level_of(own_key, shape, cuts, least, top_value):
    level, own = 1.0, jax.random.fold_in(own_key, 6)
    for dim, parts in cuts:
        steps = jnp.exp(jax.random.uniform(jax.random.fold_in(own, dim), (parts,), jnp.float32, least / len(cuts), top_value / len(cuts)))
        level = level * jnp.repeat(steps, shape[dim] // parts).reshape([-1 if axis == dim else 1 for axis in range(len(shape))])
    return level


def bell_draw(key, extent, width, limit, shards=(), held_as=jnp.bfloat16):
    loudness = level_of(key, extent, shards, -0.22, 0.18) if shards else 1.0
    values = jax.random.normal(key, extent, jnp.float32) * width * loudness
    return jnp.minimum(jnp.maximum(values, -limit), limit).astype(held_as)


def setup_inputs(seed: int = 0) -> dict:
    key_of = jax.random.split(jax.random.key(seed), 11)
    layer_input = bell_draw(key_of[0], (SEQS, LEN, MODEL_DIM), 1.0, 6.0, ((0, 128), (1, 4)))
    next_token_rows = bell_draw(key_of[1], (SEQS, LEN, MODEL_DIM), MODEL_DIM ** -0.5, 0.0625, ((0, 128), (1, 4)))
    response_length = draw_response_length(jax.random.fold_in(key_of[10], 71), 0)
    input_norm_scale = jnp.clip(1.0 + 0.18 * jax.random.normal(key_of[3], (MODEL_DIM,), jnp.float32), 0.1, 1.9)
    query_weight = bell_draw(key_of[4], (MODEL_DIM, HEAD_DIM), MODEL_DIM ** -0.5, 0.0625, ((0, 32),))
    key_weight = bell_draw(key_of[5], (MODEL_DIM, HEAD_DIM), MODEL_DIM ** -0.5, 0.0625, ((0, 32),))
    value_weight = bell_draw(key_of[6], (MODEL_DIM, HEAD_DIM), MODEL_DIM ** -0.5, 0.0625, ((0, 32),))
    output_projection_weight = bell_draw(key_of[7], (MODEL_DIM, HEAD_DIM), HEAD_DIM ** -0.5, 0.5, ((0, 32),))
    adapter_down_weight = bell_draw(key_of[8], (MODEL_DIM, ADAPTER_ORDER), MODEL_DIM ** -0.5, 0.0625, ((0, 32),))
    adapter_up_weight = bell_draw(key_of[9], (ADAPTER_ORDER, HEAD_DIM), ADAPTER_ORDER ** -0.5, 0.75)
    return dict(layer_input=layer_input, next_token_rows=next_token_rows, response_length=response_length, input_norm_scale=input_norm_scale, query_weight=query_weight, key_weight=key_weight, value_weight=value_weight, output_projection_weight=output_projection_weight, adapter_down_weight=adapter_down_weight, adapter_up_weight=adapter_up_weight)


theta_base = 500000.0
beta_dpo = 0.1
eps_norm = 1e-05

def rotate(field, position):
    half_size = field.shape[-1] // 2
    frequency = theta_base ** (-2.0 * jnp.arange(half_size, dtype=jnp.float32) / field.shape[-1])
    angles = position.astype(jnp.float32)[:, None] * frequency[None, :]
    cosine = jnp.cos(angles)
    sine_wave = jnp.sin(angles)
    first_half = field[..., :half_size]
    second_half = field[..., half_size:]
    return jnp.concatenate([first_half * cosine - second_half * sine_wave, second_half * cosine + first_half * sine_wave], axis=-1)

def normed(rows, input_norm_scale):
    wide_rows = rows.astype(jnp.float32)
    adapter_scale = lax.rsqrt(lax.optimization_barrier(jnp.mean(wide_rows * wide_rows, axis=-1, keepdims=True)) + eps_norm)
    return (wide_rows * adapter_scale * input_norm_scale).astype(jnp.bfloat16)

def layer_forward_pass(hidden_state, following_rows, response_lengths, input_norm_scale, query_weight, key_weight, value_weight, output_projection_weight, adapter_down_weight, adapter_up_weight):
    members, length, model_width = hidden_state.shape
    head_size = query_weight.shape[1]
    flat_rows = hidden_state.reshape(members * length, model_width)
    normalized_rows = normed(flat_rows, input_norm_scale)
    position = jnp.arange(length, dtype=jnp.int32)
    query = rotate(jnp.dot(normalized_rows, query_weight, preferred_element_type=jnp.float32).reshape(members, length, head_size), position).astype(jnp.bfloat16)
    all_keys = rotate(jnp.dot(normalized_rows, key_weight, preferred_element_type=jnp.float32).reshape(members, length, head_size), position).astype(jnp.bfloat16)
    frozen_value = jnp.dot(normalized_rows, value_weight, preferred_element_type=jnp.float32)
    adapter_input = jnp.dot(normalized_rows, adapter_down_weight, preferred_element_type=jnp.float32).astype(jnp.bfloat16)
    value_ref = frozen_value.astype(jnp.bfloat16)
    policy_value = (frozen_value + jnp.dot(adapter_input, adapter_up_weight, preferred_element_type=jnp.float32)).astype(jnp.bfloat16)
    values = jnp.stack([value_ref, policy_value]).reshape(2, members, length, head_size)
    scores = jnp.einsum('sqh,skh->sqk', query.astype(jnp.float32), all_keys.astype(jnp.float32)) / math.sqrt(head_size)
    allowed = position[None, :] <= position[:, None]
    scores = jnp.where(allowed[None], scores, -jnp.inf)
    attention = jax.nn.softmax(scores, axis=-1).astype(jnp.bfloat16)
    mixed_heads = jnp.einsum('sqk,mskh->msqh', attention.astype(jnp.float32), values.astype(jnp.float32)).astype(jnp.bfloat16)
    projected = jnp.dot(mixed_heads.reshape(2 * members * length, head_size), output_projection_weight.T, preferred_element_type=jnp.float32)
    resid = projected.reshape(2, members * length, model_width) + flat_rows.astype(jnp.float32)[None]
    inverse = lax.rsqrt(lax.optimization_barrier(jnp.mean(resid * resid, axis=-1, keepdims=True)) + eps_norm)
    unit_rows = resid * inverse
    target = following_rows.reshape(members * length, model_width).astype(jnp.float32)
    logits = lax.optimization_barrier(jnp.sum(unit_rows * target[None], axis=-1)).reshape(2, members, length)
    response = (position[None, :] >= length - response_lengths[:, None]).astype(jnp.float32)
    totals = lax.optimization_barrier(jnp.sum(logits * response[None], axis=-1))
    return (totals, (normalized_rows, adapter_input, attention, unit_rows[1], inverse[1], target, response))

def layer_backward_pass(saved_tensors, adapter_scale, output_projection_weight, adapter_up_weight):
    normalized_rows, adapter_input, attention, unit_pol, inverse_pol, target, response = saved_tensors
    members, length = response.shape
    head_size = output_projection_weight.shape[1]
    logit_grad = (adapter_scale[:, None] * response).reshape(members * length, 1)
    unit_grad = logit_grad * target
    resid_grad = inverse_pol * (unit_grad - unit_pol * lax.optimization_barrier(jnp.mean(unit_grad * unit_pol, axis=-1, keepdims=True)))
    head_grad = jnp.dot(resid_grad.astype(jnp.bfloat16), output_projection_weight, preferred_element_type=jnp.float32).astype(jnp.bfloat16)
    value_grad = jnp.einsum('sqk,sqh->skh', attention.astype(jnp.float32), head_grad.reshape(members, length, head_size).astype(jnp.float32))
    value_matrix_rows = value_grad.reshape(members * length, head_size).astype(jnp.bfloat16)
    up_product = jnp.dot(adapter_input.T, value_matrix_rows, preferred_element_type=jnp.float32)
    adapter_gradient = jnp.dot(value_matrix_rows, adapter_up_weight.T, preferred_element_type=jnp.float32).astype(jnp.bfloat16)
    down_product = jnp.dot(normalized_rows.T, adapter_gradient, preferred_element_type=jnp.float32)
    return (down_product, up_product)

def reference(layer_input, next_token_rows, response_length, input_norm_scale, query_weight, key_weight, value_weight, output_projection_weight, adapter_down_weight, adapter_up_weight):
    parameters = (input_norm_scale, query_weight, key_weight, value_weight, output_projection_weight, adapter_down_weight, adapter_up_weight)
    hidden_pairs = layer_input.reshape(PAIRS, 2, LEN, MODEL_DIM)
    next_pairs = next_token_rows.reshape(PAIRS, 2, LEN, MODEL_DIM)
    len_pairs = response_length.reshape(PAIRS, 2)

    def pair_totals(entry_item):
        return layer_forward_pass(entry_item[0], entry_item[1], entry_item[2], *parameters)[0]
    totals = lax.map(pair_totals, (hidden_pairs, next_pairs, len_pairs))
    model_gap = totals[:, 1, :] - totals[:, 0, :]
    margin = beta_dpo * (model_gap[:, 0] - model_gap[:, 1])
    dpo_loss = jnp.mean(jax.nn.softplus(-margin))
    chosen_weight = -beta_dpo * jax.nn.sigmoid(-margin) / PAIRS
    adapter_scale = jnp.stack([chosen_weight, -chosen_weight], axis=1)

    def scan_step(running, entry_item):
        saved_tensors = layer_forward_pass(entry_item[0], entry_item[1], entry_item[2], *parameters)[1]
        down_product, up_product = layer_backward_pass(saved_tensors, entry_item[3], output_projection_weight, adapter_up_weight)
        return ((running[0] + down_product, running[1] + up_product), None)
    zeros_init = (jnp.zeros((MODEL_DIM, ADAPTER_ORDER), jnp.float32), jnp.zeros((ADAPTER_ORDER, HEAD_DIM), jnp.float32))
    (grad_down, grad_up), ignored = lax.scan(scan_step, zeros_init, (hidden_pairs, next_pairs, len_pairs, adapter_scale))
    return (dpo_loss, grad_down, grad_up)
```

```python
import math

import jax
import jax.numpy as jnp
from jax import lax
from jax.experimental import pallas as pl
from jax.experimental.pallas import tpu as pltpu
from jax.sharding import PartitionSpec as P

theta_base = 500000.0
beta_dpo = 0.1
eps_norm = 1e-05

LAG = 2
ROUNDS = [[None, None, (0, 0, 0), (0, 0, 1), (0, 0, 0), None], [None, None, (0, 0, 1), (0, 0, 0), (0, 0, 1), None], [None, None, (7, 0, 0), (1, 0, 1), (1, 0, 1), (0, 1, 0)], [None, None, (7, 0, 1), (1, 0, 0), (7, 0, 1), (0, 1, 1)], [None, (1, 1, 1), (6, 0, 0), (2, 0, 1), (0, 2, 0), (1, 1, 1)], [None, (7, 1, 1), (6, 0, 1), (2, 0, 0), (0, 2, 1), (7, 1, 1)], [(1, 2, 1), None, (0, 3, 0), (1, 2, 1), (3, 0, 1), None], [(7, 2, 1), None, (7, 2, 1), (0, 3, 0), (5, 0, 1), None], [(2, 2, 1), (3, 1, 1), (7, 3, 0), (3, 1, 1), (2, 2, 1), (3, 1, 1)], [(5, 1, 1), (6, 2, 1), (5, 0, 1), (1, 3, 0), (6, 2, 1), (5, 1, 1)], [(4, 1, 1), (3, 2, 1), (6, 3, 0), (3, 0, 0), (3, 2, 1), (4, 1, 1)], [(7, 3, 0), (5, 2, 1), (7, 1, 0), (2, 3, 0), (5, 2, 1), (2, 2, 1)], [(4, 2, 1), (1, 3, 0), (5, 3, 0), (1, 1, 0), (4, 2, 1), (6, 2, 1)]]


def arrives(way, block):
    dy, pair, half = block
    if way < 2:
        return (dy, pair, 1 - half)
    if way == 2:
        return ((dy - 1) % 8, pair, half)
    if way == 3:
        return ((dy + 1) % 8, pair, half)
    if way == 4:
        return (dy, (1, 0, 3, 2)[pair], half)
    return (dy, (0, 2, 1, 3)[pair], half)


def dot(a, b):
    return jnp.dot(a, b, preferred_element_type=jnp.float32)


def dot_general(a, b, ca, cb):
    return lax.dot_general(a, b, (((ca,), (cb,)), ((), ())), preferred_element_type=jnp.float32)


def kernel(
    x_hbm, t_hbm, rlen, scale, wq, wk, wv, wo, wd, aup,
    loss_ref, gdown_ref, gup_ref,
    xs, ts, nx, W, acc, kv, att, vgs, vgr, vgo, mgs, mgr,
    dkeep, dsend, drecv, s1, r1y, r1z, s2y, s2z, r2y, r2z, s3, r3, s4, r4,
    us, ur, uxs, uxr, uys, uyr, uzs, uzr, ucs, ucr, ues, uer, stat,
    in_sem, ag_s, ag_r, cc_s, cc_r, kv_s, kv_r, vg_s, vg_r, mg_s, mg_r, dc_s, dc_r,
    y1_s, y1_r, z1_s, z1_r, y2_s, y2_r, z2_s, z2_r, x3_s, x3_r, c4_s, c4_r,
    uc_s, uc_r, ux_s, ux_r, uy_s, uy_r, uz_s, uz_r, ue_s, ue_r,
):
    f32, bf16 = jnp.float32, jnp.bfloat16
    dp, f, x = lax.axis_index("dp"), lax.axis_index("fsdp"), lax.axis_index("seq")
    h, y, zl, c = f // 8, f % 8, dp // 2, dp % 2
    z = h * 2 + zl

    def dev(xx, yy, zz, cc):
        return {"dp": (zz % 2) * 2 + cc, "fsdp": (zz // 2) * 8 + yy, "seq": xx}

    outer = (z + 7 + 2 * zl) % 8
    inner = (z + 1 + 6 * zl) % 8
    sib = dev(x, y, z, 1 - c)
    ways = [
        dev((x + 1) % 4, y, z, c),
        dev((x + 3) % 4, y, z, c),
        dev(x, (y + 1) % 8, z, c),
        dev(x, (y + 7) % 8, z, c),
        dev(x, y, outer, c),
        dev(x, y, inner, c),
    ]

    def remote(src, dst, ss, rs, to):
        return pltpu.make_async_remote_copy(src_ref=src, dst_ref=dst, send_sem=ss, recv_sem=rs, device_id=to)

    in_x = pltpu.make_async_copy(x_hbm, xs, in_sem.at[0])
    in_t = pltpu.make_async_copy(t_hbm, ts, in_sem.at[1])
    in_x.start()
    in_t.start()

    for k, w in enumerate((wq, wk, wv, wo)):
        W[f, k * 288 : k * 288 + 256, :] = w[...]
        W[f, k * 288 + 256 : k * 288 + 288, 0:64] = wd[k * 32 : k * 32 + 32, :]
        W[f, k * 288 + 256 : k * 288 + 288, 64:128] = wd[128 + k * 32 : 160 + k * 32, :]
    kv[...] = jnp.zeros_like(kv)
    acc[...] = jnp.zeros_like(acc)

    barrier = pltpu.get_barrier_semaphore()
    greet = [sib]
    greet += [dev((x + o) % 4, y, z, c) for o in (1, 2, 3)]
    greet += [dev(x, (y + o) % 8, z, c) for o in range(1, 8)]
    greet += [dev(x, y, (z + o) % 8, c) for o in range(1, 8)]
    other = z + 1 - 2 * zl
    greet += [dev(x, (y + o) % 8, other, c) for o in range(1, 8)]
    for to in greet:
        pl.semaphore_signal(barrier, inc=1, device_id=to)
    pl.semaphore_wait(barrier, len(greet))

    pairs = [h, (h + 3 + 2 * zl) % 4, (h + 1 + 2 * (1 - zl) * 0 + 2 * zl) % 4, (h + 2) % 4]
    pairs[1] = (h + 3 + 2 * zl) % 4
    pairs[2] = (h + 1 + 2 * zl) % 4

    def region(block, core):
        dy, pair, half = block
        rows = (core * 2 + (half + x) % 2) * 288
        return W.at[pairs[pair] * 8 + (y + dy) % 8, pl.ds(pl.multiple_of(rows, 16), 288), :]

    sends, shares, when_in = {}, {}, {}
    for r, row in enumerate(ROUNDS):
        for d, block in enumerate(row):
            if block is not None:
                a = region(block, c)
                sends[r, d] = remote(a, a, ag_s.at[r, d], ag_r.at[r, d], ways[d])
                got = arrives(d, block)
                b = region(got, c)
                shares[r, d] = remote(b, b, cc_s.at[r, d], cc_r.at[r, d], sib)
                when_in[got] = (r, d)

    def norm_rows():
        in_x.wait()
        in_t.wait()
        width = 1024

        def sums(i, carry):
            xx, xt = carry
            cols = pl.ds(pl.multiple_of(i * width, width), width)
            a = xs[:, cols].astype(f32)
            b = ts[:, cols].astype(f32)
            return xx + jnp.sum(a * a, axis=1, keepdims=True), xt + jnp.sum(a * b, axis=1, keepdims=True)

        zero = jnp.zeros((128, 1), f32)
        xx, xt = lax.fori_loop(0, 8192 // width, sums, (zero, zero))
        stat[0] = jnp.broadcast_to(xx, (128, 128))
        stat[1] = jnp.broadcast_to(xt, (128, 128))
        inv = lax.rsqrt(xx / 8192.0 + eps_norm)

        def rows(i, carry):
            cols = pl.ds(pl.multiple_of(i * width, width), width)
            nx[:, cols] = (xs[:, cols].astype(f32) * inv * scale[:, cols]).astype(bf16)
            return carry

        lax.fori_loop(0, 8192 // width, rows, 0)
        lane = lax.broadcasted_iota(jnp.int32, (128, 128), 1)
        token = lax.broadcasted_iota(jnp.int32, (128, 128), 0)
        position = (x * 64 + token % 64).astype(f32)
        rate = jnp.exp((lane % 64).astype(f32) * (-2.0 / 128.0 * math.log(theta_base)))
        angle = position * rate
        stat[2] = jnp.cos(angle)
        sine = jnp.sin(angle)
        stat[3] = jnp.where(lane < 64, -sine, sine)

    def multiply(dy):
        def body(hh, carry):
            g = hh * 8 + (y + dy) % 8
            cols = pl.ds(pl.multiple_of(g * 256, 256), 256)
            a, raw, tgt = nx[:, cols], xs[:, cols], ts[:, cols]
            qk = jnp.concatenate([W[g, 0:256, :], W[g, 288:544, :]], axis=1)
            out = W[g, 864:1120, :]
            down = jnp.concatenate([W[g, 288 * k + 256 : 288 * k + 288, :] for k in range(4)], axis=0)
            both = dot(a, qk)
            acc[0] += both[:, 0:128]
            acc[1] += both[:, 128:256]
            acc[2] += dot(a, W[g, 576:832, :])
            acc[3] += dot(a[:, 0:128], down)
            acc[4] += dot(a[:, 128:256], down)
            acc[5] += dot(raw, out)
            acc[6] += dot(tgt, out)
            acc[7] += dot_general(out, out, 0, 0)
            return carry

        lax.fori_loop(0, 4, body, 0)

    last = {}
    for block, (r, d) in when_in.items():
        last[block[0]] = max(last.get(block[0], 0), r)
    for r in range(len(ROUNDS) + LAG + 1):
        if r >= LAG:
            for d in range(6):
                if (r - LAG, d) in sends:
                    sends[r - LAG, d].wait_recv()
        for d in range(6):
            if (r, d) in sends:
                sends[r, d].start()
        if r >= LAG:
            for d in range(6):
                if (r - LAG, d) in sends:
                    shares[r - LAG, d].start()
        if r == LAG - 1:
            norm_rows()
        for dy in range(8):
            if last[dy] == r - LAG - 1:
                for block, where in when_in.items():
                    if block[0] == dy:
                        shares[where].wait_recv()
                multiply(dy)

    def rope(v):
        return (v * stat[2] + pltpu.roll(v, 64, 1) * stat[3]).astype(bf16)

    q = rope(acc[0])
    own = pl.ds(pl.multiple_of(x * 64, 64), 64)
    d_in = (acc[3][:, 0:64] + acc[4][:, 64:128]).astype(bf16)
    base = acc[2]
    k_own = rope(acc[1])
    v_ref = base.astype(bf16)
    v_pol = (base + dot(d_in, aup[...])).astype(bf16)
    for b in range(2):
        kv[0, b, own, :] = k_own[b * 64 : b * 64 + 64]
        kv[1, b, own, :] = v_ref[b * 64 : b * 64 + 64]
        kv[2, b, own, :] = v_pol[b * 64 : b * 64 + 64]
    kv_own = kv.at[:, :, own, :]
    kvs = [remote(kv_own, kv_own, kv_s.at[o], kv_r.at[o], dev((x + o) % 4, y, z, c)) for o in range(4)]
    for o in (1, 2, 3):
        @pl.when(x + o < 4)
        def _():
            kvs[o].start()

    g_hi = acc[7].astype(bf16)
    g_lo = (acc[7] - g_hi.astype(f32)).astype(bf16)
    for key in sends:
        sends[key].wait_send()
        shares[key].wait_send()
    for o in (1, 2, 3):
        @pl.when(x - o >= 0)
        def _():
            kvs[o].wait_recv()

    row = lax.broadcasted_iota(jnp.int32, (64, 256), 0)
    col = lax.broadcasted_iota(jnp.int32, (64, 256), 1)
    allowed = col <= row + x * 64
    mixed = [[], []]
    for b in range(2):
        s = dot_general(q[b * 64 : b * 64 + 64], kv[0, b], 1, 1) / math.sqrt(128.0)
        s = jnp.where(allowed, s, -1e30)
        e = jnp.exp(s - jnp.max(s, axis=1, keepdims=True))
        e = jnp.where(allowed, e, 0.0)
        w = (e / jnp.sum(e, axis=1, keepdims=True)).astype(bf16)
        att[b] = w
        for m in range(2):
            mixed[m].append(dot(w, kv[1 + m, b]).astype(bf16))

    xx, xt, po, to = stat[0][:, 0:1], stat[1][:, 0:1], acc[5], acc[6]
    logits, invs, projs = [], [], []
    for m in range(2):
        mix = jnp.concatenate(mixed[m], axis=0)
        mg = dot(mix, g_hi) + dot(mix, g_lo)
        mixf = mix.astype(f32)
        sq = xx + jnp.sum(mixf * (2.0 * po + mg), axis=1, keepdims=True)
        inv = lax.rsqrt(sq / 8192.0 + eps_norm)
        logits.append(inv * (xt + jnp.sum(mixf * to, axis=1, keepdims=True)))
        invs.append(inv)
        projs.append(po + mg)
    token = lax.broadcasted_iota(jnp.int32, (128, 1), 0)
    start = jnp.where(token < 64, 256 - rlen[0], 256 - rlen[1])
    sign = jnp.where(token < 64, 1.0, -1.0)
    resp = jnp.where(x * 64 + token % 64 >= start, sign, 0.0)
    part = jnp.sum(resp * (logits[1] - logits[0]), axis=0, keepdims=True)
    mgs[...] = jnp.broadcast_to(part, (8, 128))
    mgc = [remote(mgs, mgr.at[o], mg_s.at[o], mg_r.at[o], dev((x + o) % 4, y, z, c)) for o in range(4)]
    for o in (1, 2, 3):
        mgc[o].start()

    head = (resp * invs[1] * (to - (logits[1] / 8192.0) * invs[1] * projs[1])).astype(bf16)
    for b in range(2):
        terms = dot_general(att[b], head[b * 64 : b * 64 + 64], 0, 0)
        vgs[b] = terms.astype(bf16)
        vgo[b] = terms
    vgc = []
    for o in range(4):
        target = (x + 4 - o) % 4
        src = vgs.at[:, pl.ds(pl.multiple_of(target * 64, 64), 64), :]
        vgc.append(remote(src, vgr.at[o], vg_s.at[o], vg_r.at[o], dev(target, y, z, c)))
    for o in (1, 2, 3):
        @pl.when(x - o >= 0)
        def _():
            vgc[o].start()
    for o in (1, 2, 3):
        mgc[o].wait()
    margin = beta_dpo * (mgs[...] + mgr[1] + mgr[2] + mgr[3])
    pull = (-beta_dpo / 128.0) / (1.0 + jnp.exp(margin))
    loss = jnp.maximum(-margin, 0.0) + jnp.log1p(jnp.exp(-jnp.abs(margin)))
    mine = [vgo[b, own, :] for b in range(2)]
    total = jnp.concatenate(mine, axis=0)
    vgo[0, 0:128, :] = total
    for o in (1, 2, 3):
        @pl.when(x + o < 4)
        def _():
            vgc[o].wait_recv()
            vgo[0, 0:128, :] += vgr[o].reshape(128, 128).astype(f32)
    vg = (vgo[0, 0:128, :] * pull[0:1, :]).astype(bf16)

    up = dot_general(d_in, vg, 0, 0)
    agt = dot_general(aup[...], vg, 1, 1).astype(bf16)

    us[...] = up
    keep = pl.ds(pl.multiple_of(c * 32, 32), 32)
    give = pl.ds(pl.multiple_of(32 - c * 32, 32), 32)
    ucs[32:40, :] = loss
    ucs[0:32, :] = us[give, :]
    uc = remote(ucs, ucr, uc_s.at[0], uc_r.at[0], sib)
    uc.start()

    ag_keep = jnp.where(c == 0, agt[0:32], agt[32:64])
    ag_give = jnp.where(c == 0, agt[32:64], agt[0:32])
    dcs = []
    for n in range(4):
        def give_body(i, carry):
            g = n * 8 + i
            cols = pl.ds(pl.multiple_of(g * 256, 256), 256)
            dsend[g] = dot(ag_give, nx[:, cols]).astype(bf16)
            return carry
        lax.fori_loop(0, 8, give_body, 0)
        cp = remote(dsend.at[pl.ds(n * 8, 8)], drecv.at[pl.ds(n * 8, 8)], dc_s.at[n], dc_r.at[n], sib)
        cp.start()
        dcs.append(cp)

    def keep_body(g, carry):
        cols = pl.ds(pl.multiple_of(g * 256, 256), 256)
        dkeep[g] = dot(ag_keep, nx[:, cols])
        return carry
    lax.fori_loop(0, 32, keep_body, 0)

    uc.wait()
    uxs[0:32, :] = us[keep, :] + ucr[0:32, :]
    uxs[32:40, :] = loss + ucr[32:40, :]
    uxc = [remote(uxs, uxr.at[o], ux_s.at[o], ux_r.at[o], dev((x + o) % 4, y, z, c)) for o in range(4)]
    for o in (1, 2, 3):
        uxc[o].start()

    for n in range(4):
        dcs[n].wait_recv()
        def add_body(i, carry):
            g = n * 8 + i
            s1[n, i] = (dkeep[g] + drecv[g].astype(f32)).astype(bf16)
            return carry
        lax.fori_loop(0, 8, add_body, 0)

    y1, z1 = [], []
    for o in range(8):
        ty, tz = (y + o) % 8, (z + o) % 8
        y1.append(remote(s1.at[:, ty, pl.ds(0, 16), :], r1y.at[o], y1_s.at[o], y1_r.at[o], dev(x, ty, z, c)))
        z1.append(remote(s1.at[tz // 2, pl.ds((tz % 2) * 4, 4), pl.ds(16, 16), :], r1z.at[o], z1_s.at[o], z1_r.at[o],
                         dev(x, y, tz, c)))
    for o in (4, 3, 5, 2, 6, 1, 7):
        y1[o].start()
        z1[o].start()
    for o in (1, 2, 3):
        uxc[o].wait()
    uys[...] = uxs[...] + uxr[1] + uxr[2] + uxr[3]
    uyc = [remote(uys, uyr.at[o], uy_s.at[o], uy_r.at[o], dev(x, (y + o) % 8, z, c)) for o in range(8)]
    for o in range(1, 8):
        uyc[o].start()
    for o in range(1, 8):
        y1[o].wait()
        z1[o].wait()
    sy = s1[:, y, 0:16, :].astype(f32)
    sz = s1[h, pl.ds(zl * 4, 4), 16:32, :].astype(f32)
    for o in range(1, 8):
        sy += r1y[o].astype(f32)
        sz += r1z[o].astype(f32)
    s2y[...] = sy.astype(bf16)
    s2z[...] = sz.astype(bf16)

    y2 = []
    for o in range(8):
        tz = (z + o) % 8
        y2.append(remote(s2y.at[tz // 2], r2y.at[o], y2_s.at[o], y2_r.at[o], dev(x, y, tz, c)))
    for o in range(1, 8):
        y2[o].start()
    z2 = []
    for j in range(4):
        for zz in range(2):
            ty = zl * 4 + j
            z2.append((remote(s2z.at[j], r2z.at[y], z2_s.at[j * 2 + zz], z2_r.at[y], dev(x, ty, h * 2 + zz, c)),
                       jnp.logical_and(ty == y, zz == zl), j))
    for cp, me, j in z2:
        @pl.when(jnp.logical_not(me))
        def _():
            cp.start()
        @pl.when(me)
        def _():
            r2z[y] = s2z[j]
    for o in range(1, 8):
        uyc[o].wait()
    tot = uys[...]
    for o in range(1, 8):
        tot += uyr[o]
    uzs[...] = tot
    uzc = [remote(uzs, uzr.at[o], uz_s.at[o], uz_r.at[o], dev(x, y, (z + o) % 8, c)) for o in range(8)]
    for o in range(1, 8):
        uzc[o].start()
    for o in range(1, 8):
        y2[o].wait()
    for cp, me, j in z2:
        @pl.when(jnp.logical_not(me))
        def _():
            cp.wait_send()
    for s in range(8):
        @pl.when(jnp.logical_not(jnp.logical_and(s == y, y // 4 == zl)))
        def _():
            remote(s2z.at[0], r2z.at[s], z2_s.at[0], z2_r.at[s], sib).wait_recv()
    ty_ = s2y[h].astype(f32)
    tz_ = r2z[0].astype(f32)
    for o in range(1, 8):
        ty_ += r2y[o].astype(f32)
        tz_ += r2z[o].astype(f32)
    for k in range(2):
        s3[k, 0:16, :] = ty_[:, k * 128 : k * 128 + 128]
        s3[k, 16:32, :] = tz_[:, k * 128 : k * 128 + 128]

    x3 = []
    for o in range(4):
        tx = (x + o) % 4
        x3.append(remote(s3.at[tx // 2], r3.at[o], x3_s.at[o], x3_r.at[o], dev(tx, y, z, c)))
    for o in (1, 2, 3):
        x3[o].start()
    for o in range(1, 8):
        uzc[o].wait()
    tot = uzs[...]
    for o in range(1, 8):
        tot += uzr[o]
    ues[...] = tot[0:32, :]
    ue = remote(ues, uer, ue_s.at[0], ue_r.at[0], sib)
    ue.start()
    loss_ref[...] = tot[32:40, :] * (1.0 / 512.0)
    for o in (1, 2, 3):
        x3[o].wait()
    mine = s3[x // 2] + r3[1] + r3[2] + r3[3]
    s4[...] = mine
    c4 = remote(s4, r4, c4_s.at[0], c4_r.at[0], sib)
    c4.start()
    ue.wait()
    gup_ref[keep, :] = ues[...]
    gup_ref[give, :] = uer[...]
    for o in (1, 2, 3):
        @pl.when(x + o < 4)
        def _():
            kvs[o].wait_send()
        @pl.when(x - o >= 0)
        def _():
            vgc[o].wait_send()
    for n in range(4):
        dcs[n].wait_send()
    c4.wait()
    low = jnp.where(c == 0, s4[...], r4[...])
    high = jnp.where(c == 0, r4[...], s4[...])
    whole = jnp.concatenate([low, high], axis=0)
    whole = jnp.where(x % 2 == 0, whole, pltpu.roll(whole, 64, 1))
    gdown_ref[...] = whole.T[0:64, :]


def step(x_in, t_in, rlen, scale, wq, wk, wv, wo, wd, aup):
    f32, bf16 = jnp.float32, jnp.bfloat16
    V = pltpu.VMEM
    D = pltpu.SemaphoreType.DMA
    n = len(ROUNDS)
    vm = pl.BlockSpec(memory_space=pltpu.VMEM)
    hb = pl.BlockSpec(memory_space=pl.ANY)
    loss, gdown, gup = pl.pallas_call(
        kernel,
        name="dpo_step",
        out_shape=(
            jax.ShapeDtypeStruct((8, 128), f32),
            jax.ShapeDtypeStruct((64, 64), f32),
            jax.ShapeDtypeStruct((64, 128), f32),
        ),
        in_specs=[hb, hb, pl.BlockSpec(memory_space=pltpu.SMEM)] + [vm] * 7,
        out_specs=(vm, vm, vm),
        scratch_shapes=[
            V((128, 8192), bf16), V((128, 8192), bf16), V((128, 8192), bf16),
            V((32, 1152, 128), bf16), V((8, 128, 128), f32), V((3, 2, 256, 128), bf16), V((2, 64, 256), bf16),
            V((2, 256, 128), bf16), V((4, 2, 64, 128), bf16), V((2, 256, 128), f32), V((8, 128), f32), V((4, 8, 128), f32),
            V((32, 32, 256), f32), V((32, 32, 256), bf16), V((32, 32, 256), bf16), V((4, 8, 32, 256), bf16),
            V((8, 4, 16, 256), bf16), V((8, 4, 16, 256), bf16), V((4, 16, 256), bf16), V((4, 16, 256), bf16),
            V((8, 16, 256), bf16), V((8, 16, 256), bf16), V((2, 32, 128), f32), V((4, 32, 128), f32),
            V((32, 128), f32), V((32, 128), f32),
            V((64, 128), f32), V((64, 128), f32), V((40, 128), f32), V((4, 40, 128), f32), V((40, 128), f32),
            V((8, 40, 128), f32), V((40, 128), f32), V((8, 40, 128), f32), V((40, 128), f32), V((40, 128), f32), V((32, 128), f32), V((32, 128), f32),
            V((4, 128, 128), f32),
            D((2,)), D((n, 6)), D((n, 6)), D((n, 6)), D((n, 6)), D((4,)), D((4,)), D((4,)), D((4,)), D((4,)), D((4,)),
            D((4,)), D((4,)), D((8,)), D((8,)), D((8,)), D((8,)), D((8,)), D((8,)), D((8,)), D((8,)), D((4,)), D((4,)),
            D((1,)), D((1,)), D((1,)), D((1,)), D((4,)), D((4,)), D((8,)), D((8,)), D((8,)), D((8,)), D((1,)), D((1,)),
        ],
        compiler_params=pltpu.CompilerParams(
            collective_id=0, has_side_effects=True, vmem_limit_bytes=56 * 2**20
        ),
    )(
        x_in.reshape(128, 8192), t_in.reshape(128, 8192), rlen, scale.reshape(1, 8192), wq, wk, wv, wo, wd, aup
    )
    return loss[0, 0], gdown, gup


def solution(mesh):
    return jax.shard_map(
        step,
        mesh=mesh,
        in_specs=(
            P(("dp", "fsdp"), "seq", None),
            P(("dp", "fsdp"), "seq", None),
            P(("dp", "fsdp")),
            P(),
            P("fsdp", None),
            P("fsdp", None),
            P("fsdp", None),
            P("fsdp", None),
            P("fsdp", None),
            P(),
        ),
        out_specs=(P(), P(("fsdp", "seq"), None), P()),
        check_vma=False,
    )
```

```python
import math

import jax
import jax.numpy as jnp
from jax import lax
from jax.experimental import pallas as pl
from jax.experimental.pallas import tpu as pltpu
from jax.sharding import PartitionSpec as P

theta_base = 500000.0
beta_dpo = 0.1
eps_norm = 1e-05

PARTS = 2
SENDS = 124
GATHER = (
    (0,4,0,0,1,0), (0,3,0,0,0,0), (0,2,0,0,1,1), (0,2,0,0,0,0), (0,3,0,0,0,1), (0,4,0,0,0,1), (0,3,0,0,1,0),
    (0,4,0,0,1,1), (0,2,0,0,0,1), (2,), (0,3,0,0,1,1), (0,2,0,0,1,0), (0,4,0,0,0,0), (1,0), (0,5,0,1,1,0), (1,2),
    (0,2,7,0,1,1), (1,1), (0,3,1,0,0,0), (0,4,1,0,0,0), (1,5), (0,5,0,1,0,1), (1,4), (0,3,1,0,0,1), (0,4,7,0,1,1),
    (1,3), (0,2,7,0,0,0), (1,7), (0,5,0,1,1,1), (0,2,0,1,1,0), (0,4,1,0,0,1), (1,6), (0,3,1,0,1,0), (1,11),
    (0,5,0,1,0,0), (1,9), (0,3,1,0,1,1), (1,10), (0,2,7,0,1,0), (1,8), (0,4,7,0,0,1), (1,15), (0,5,1,1,0,0), (1,13),
    (0,0,6,0,1,1), (0,1,1,1,0,0), (0,2,6,0,1,1), (1,14), (0,3,2,0,0,0), (1,12), (0,4,0,2,1,0), (1,18), (0,5,7,1,1,1),
    (1,19), (0,2,6,0,0,0), (1,17), (0,3,2,0,0,1), (1,16), (0,4,0,2,0,1), (1,21), (0,5,7,1,1,0), (1,22),
    (0,1,1,1,0,1), (0,0,7,1,1,0), (0,2,7,1,1,0), (1,23), (0,4,2,0,1,0), (1,20), (0,3,0,2,1,1), (1,27), (0,5,7,1,0,1),
    (3,0,1,4,28), (0,2,7,1,0,1), (0,3,1,1,0,1), (0,4,0,2,1,1), (1,28), (0,0,1,2,0,0), (0,5,1,1,0,1), (1,33),
    (0,1,0,3,1,0), (0,2,0,3,1,0), (0,3,1,2,0,0), (0,4,1,2,0,0), (1,24), (1,25), (1,26), (1,31), (0,0,5,0,1,1),
    (1,36), (0,1,3,0,0,1), (1,37), (0,3,0,3,0,1), (1,34), (0,2,7,2,1,1), (0,4,7,2,1,1), (1,29), (1,30), (1,32),
    (1,40), (0,5,7,1,0,0), (1,35), (0,0,5,0,0,0), (0,1,3,0,0,0), (1,41), (0,2,6,1,1,0), (1,43), (0,3,1,2,1,1),
    (0,4,3,0,0,0), (0,5,6,1,1,0), (0,0,6,1,1,0), (1,46), (0,1,2,1,0,1), (0,2,5,0,1,1), (0,4,5,0,1,1), (0,3,0,3,1,0),
    (1,38), (1,39), (1,42), (1,45), (0,0,6,1,0,1), (0,5,6,1,0,1), (1,51), (0,1,7,3,1,0), (0,2,7,3,1,0),
    (0,4,3,0,0,1), (1,52), (0,3,2,2,0,0), (1,44), (1,47), (0,0,2,2,0,0), (0,5,2,1,0,1), (1,56), (0,1,1,3,0,1),
    (0,3,1,3,0,1), (1,58), (0,2,7,3,1,1), (0,4,2,2,0,0), (1,48), (1,49), (1,50), (1,53), (0,5,2,2,0,0),
    (3,2,8,24,29), (0,0,7,3,1,1), (1,62), (0,1,5,1,1,0), (1,55), (0,4,3,0,1,1), (1,63), (0,3,2,2,1,1), (0,2,5,1,1,0),
    (1,54), (1,57), (1,65), (0,0,6,2,1,0), (0,5,5,1,1,0), (1,68), (0,1,4,0,1,1), (0,4,2,2,1,1), (0,2,6,2,1,1),
    (0,3,3,0,0,0), (1,59), (1,60), (1,61), (1,64), (1,69), (0,0,5,1,1,1), (1,75), (0,5,3,1,0,1), (1,76),
    (0,1,3,2,0,0), (0,4,3,2,0,0), (1,74), (0,2,6,3,1,0), (0,3,3,2,0,0), (1,66), (1,67), (1,70), (0,0,6,3,1,0),
    (1,81), (0,1,6,3,1,1), (0,4,4,0,1,1), (0,2,6,3,1,1), (1,80), (0,3,2,3,0,1), (1,71), (1,72), (1,73), (1,85),
    (0,5,5,1,0,0), (1,82), (0,0,2,3,0,0), (1,88), (0,1,4,1,1,0), (1,87), (0,4,3,2,1,1), (0,2,6,2,0,1), (0,3,3,2,1,1),
    (1,77), (1,78), (1,79), (0,5,4,1,1,0), (0,0,3,1,0,0), (1,94), (0,1,4,0,0,0), (1,91), (0,4,4,0,0,1), (1,83),
    (1,84), (1,86), (1,96), (0,3,3,2,0,1), (3,3,5,6,12,20,30), (1,99), (0,2,5,3,1,0), (0,0,5,3,1,0), (1,98),
    (0,1,3,3,0,0), (1,100), (0,4,4,2,0,0), (1,89), (1,90), (1,92), (1,93), (1,105), (0,3,3,3,0,1), (1,104),
    (0,0,5,3,1,1), (0,2,5,3,1,1), (1,95), (1,97), (1,101), (1,102), (1,103), (1,106), (1,107), (1,108), (1,109),
    (1,110), (1,111), (1,112), (1,113), (1,114), (1,115), (1,116), (1,117), (1,118), (1,119), (1,120), (1,121),
    (1,122), (1,123), (3,7,9,10,11,13,14,15,16,17,18,19,21,22,23,25,26,27,31),
)

def arrives(way, piece):
    dy, pair, half, part = piece
    if way < 2:
        return (dy, pair, 1 - half, part)
    if way == 2:
        return ((dy - 1) % 8, pair, half, part)
    if way == 3:
        return ((dy + 1) % 8, pair, half, part)
    if way == 4:
        return (dy, (1, 0, 3, 2)[pair], half, part)
    return (dy, (0, 2, 1, 3)[pair], half, part)

def dot(a, b):
    return jnp.dot(a, b, preferred_element_type=jnp.float32)

def dot_general(a, b, ca, cb):
    return lax.dot_general(a, b, (((ca,), (cb,)), ((), ())), preferred_element_type=jnp.float32)

def kernel(
    x_hbm, t_hbm, rlen, scale, wq, wk, wv, wo, wd, aup,
    out_ref,
    xs, ts, nx, W, acc, kv, att, vgs, vgr, vgo, mgs, mgr,
    dkeep, dsend, drecv, s1, r1y, r1z, s2y, s2z, r2y, r2z, s3, r3, s4, r4,
    us, ur, uxs, uxr, uys, uyr, uzs, uzr, ucs, ucr, ues, uer, stat,
    in_sem, ag_s, ag_r, cc_s, cc_r, kv_s, kv_r, vg_s, vg_r, mg_s, mg_r, dc_s, dc_r,
    y1_s, y1_r, z1_s, z1_r, y2_s, y2_r, z2_s, z2_r, x3_s, x3_r, c4_s, c4_r,
    uc_s, uc_r, ux_s, ux_r, uy_s, uy_r, uz_s, uz_r, ue_s, ue_r,
):
    f32, bf16 = jnp.float32, jnp.bfloat16
    dp, f, x = lax.axis_index("dp"), lax.axis_index("fsdp"), lax.axis_index("seq")
    h, y, zl, c = f // 8, f % 8, dp // 2, dp % 2
    z = h * 2 + zl

    def dev(xx, yy, zz, cc):
        return {"dp": (zz % 2) * 2 + cc, "fsdp": (zz // 2) * 8 + yy, "seq": xx}

    outer = (z + 7 + 2 * zl) % 8
    inner = (z + 1 + 6 * zl) % 8
    sib = dev(x, y, z, 1 - c)
    ways = [
        dev((x + 1) % 4, y, z, c),
        dev((x + 3) % 4, y, z, c),
        dev(x, (y + 1) % 8, z, c),
        dev(x, (y + 7) % 8, z, c),
        dev(x, y, outer, c),
        dev(x, y, inner, c),
    ]

    def remote(src, dst, ss, rs, to):
        return pltpu.make_async_remote_copy(src_ref=src, dst_ref=dst, send_sem=ss, recv_sem=rs, device_id=to)

    in_x = pltpu.make_async_copy(x_hbm, xs, in_sem.at[0])
    in_t = pltpu.make_async_copy(t_hbm, ts, in_sem.at[1])
    in_x.start()
    in_t.start()

    for k, w in enumerate((wq, wk, wv, wo)):
        W[f, k * 288 : k * 288 + 256, :] = w[...]
        W[f, k * 288 + 256 : k * 288 + 288, :] = wd[(k % 2) * 32 : (k % 2) * 32 + 32, (k // 2) * 128 : (k // 2) * 128 + 128]
    kv[...] = jnp.zeros_like(kv)
    acc[...] = jnp.zeros_like(acc)

    barrier = pltpu.get_barrier_semaphore()
    greet = [sib]
    greet += [dev((x + o) % 4, y, z, c) for o in (1, 2, 3)]
    greet += [dev(x, (y + o) % 8, z, c) for o in range(1, 8)]
    greet += [dev(x, y, (z + o) % 8, c) for o in range(1, 8)]
    other = z + 1 - 2 * zl
    greet += [dev(x, (y + o) % 8, other, c) for o in range(1, 8)]
    for to in greet:
        pl.semaphore_signal(barrier, inc=1, device_id=to)
    pl.semaphore_wait(barrier, len(greet))

    pairs = [h, (h + 3 + 2 * zl) % 4, (h + 1 + 2 * (1 - zl) * 0 + 2 * zl) % 4, (h + 2) % 4]
    pairs[1] = (h + 3 + 2 * zl) % 4
    pairs[2] = (h + 1 + 2 * zl) % 4

    def region(piece):
        dy, pair, half, part = piece
        rows = (c * 2 + (half + x) % 2) * 288 + part * (288 // PARTS)
        return W.at[pairs[pair] * 8 + (y + dy) % 8, pl.ds(pl.multiple_of(rows, 16), 288 // PARTS), :]

    groups = [do[1:] for do in GATHER if do[0] == 3]
    group_of = {block: k for k, blocks in enumerate(groups) for block in blocks}
    sends, came = [], []
    for do in GATHER:
        if do[0] == 0:
            n = len(sends)
            a = region(do[2:])
            came.append(arrives(do[1], do[2:]))
            sends.append(remote(a, a, ag_s.at[0], ag_r.at[n], ways[do[1]]))

    def half_block(dy, pair, half):
        rows = (c * 2 + (half + x) % 2) * 288
        return W.at[pairs[pair] * 8 + (y + dy) % 8, pl.ds(pl.multiple_of(rows, 16), 288), :]

    def whole(blocks, sem):
        ref = W.at[pl.ds(0, blocks), pl.ds(0, 576), :]
        return pltpu.make_async_copy(ref, ref, sem)

    parts_in = {}

    def arrive(n):
        dy, pair, half, _ = came[n]
        sends[n].wait_recv()
        parts_in[dy, pair, half] = parts_in.get((dy, pair, half), 0) + 1
        if parts_in[dy, pair, half] == PARTS:
            a = half_block(dy, pair, half)
            remote(a, a, cc_s.at[0], cc_r.at[group_of[dy * 4 + pair]], sib).start()

    def norm_rows():
        in_x.wait()
        in_t.wait()
        width = 1024

        def sums(i, carry):
            xx, xt = carry
            cols = pl.ds(pl.multiple_of(i * width, width), width)
            a = xs[:, cols].astype(f32)
            b = ts[:, cols].astype(f32)
            return xx + jnp.sum(a * a, axis=1, keepdims=True), xt + jnp.sum(a * b, axis=1, keepdims=True)

        zero = jnp.zeros((128, 1), f32)
        xx, xt = lax.fori_loop(0, 8192 // width, sums, (zero, zero))
        stat[0] = jnp.broadcast_to(xx, (128, 128))
        stat[1] = jnp.broadcast_to(xt, (128, 128))
        inv = lax.rsqrt(xx / 8192.0 + eps_norm)

        def rows(i, carry):
            cols = pl.ds(pl.multiple_of(i * width, width), width)
            nx[:, cols] = (xs[:, cols].astype(f32) * inv * scale[:, cols]).astype(bf16)
            return carry

        lax.fori_loop(0, 8192 // width, rows, 0)
        lane = lax.broadcasted_iota(jnp.int32, (128, 128), 1)
        token = lax.broadcasted_iota(jnp.int32, (128, 128), 0)
        position = (x * 64 + token % 64).astype(f32)
        rate = jnp.exp((lane % 64).astype(f32) * (-2.0 / 128.0 * math.log(theta_base)))
        angle = position * rate
        stat[2] = jnp.cos(angle)
        sine = jnp.sin(angle)
        stat[3] = jnp.where(lane < 64, -sine, sine)

    def multiply(blocks):
        whole(len(blocks) - (0 in blocks), cc_r.at[group_of[blocks[0]]]).wait()

        def body(i, carry):
            g = jnp.int32(0)
            for k, block in enumerate(blocks):
                g += jnp.where(i == k, 1, 0) * (pairs[block % 4] * 8 + (y + block // 4) % 8)
            cols = pl.ds(pl.multiple_of(g * 256, 256), 256)
            a, raw, tgt = nx[:, cols], xs[:, cols], ts[:, cols]
            qk = jnp.concatenate([W[g, 0:256, :], W[g, 288:544, :]], axis=1)
            out = W[g, 864:1120, :]
            down = jnp.concatenate(
                [jnp.concatenate([W[g, 288 * k + 256 : 288 * k + 288, :] for k in (k0, k0 + 1)], axis=0) for k0 in (0, 2)],
                axis=1,
            )
            both = dot(a, qk)
            acc[0] += both[:, 0:128]
            acc[1] += both[:, 128:256]
            acc[2] += dot(a, W[g, 576:832, :])
            acc[3, :, 0:64] += dot_general(a, down, 1, 1)
            acc[5] += dot(raw, out)
            acc[6] += dot(tgt, out)
            acc[7] += dot_general(out, out, 0, 0)
            return carry

        lax.fori_loop(0, len(blocks), body, 0, unroll=2)

    n = 0
    for do in GATHER:
        if do[0] == 0:
            sends[n].start()
            n += 1
        elif do[0] == 1:
            arrive(do[1])
        elif do[0] == 2:
            norm_rows()
        else:
            multiply(do[1:])

    def rope(v):
        return (v * stat[2] + pltpu.roll(v, 64, 1) * stat[3]).astype(bf16)

    q = rope(acc[0])
    own = pl.ds(pl.multiple_of(x * 64, 64), 64)
    d_in = acc[3, :, 0:64].astype(bf16)
    base = acc[2]
    k_own = rope(acc[1])
    v_ref = base.astype(bf16)
    v_pol = (base + dot(d_in, aup[...])).astype(bf16)
    for b in range(2):
        kv[0, b, own, :] = k_own[b * 64 : b * 64 + 64]
        kv[1, b, own, :] = v_ref[b * 64 : b * 64 + 64]
        kv[2, b, own, :] = v_pol[b * 64 : b * 64 + 64]
    kv_own = kv.at[:, :, own, :]
    kvs = [remote(kv_own, kv_own, kv_s.at[o], kv_r.at[o], dev((x + o) % 4, y, z, c)) for o in range(4)]
    for o in (1, 2, 3):
        @pl.when(x + o < 4)
        def _():
            kvs[o].start()

    def waitkv():
        for o in (1, 2, 3):
            @pl.when(x + o < 4)
            def _():
                kvs[o].wait_send()

    def waitvg():
        for o in (1, 2, 3):
            @pl.when(x - o >= 0)
            def _():
                vgc[o].wait_send()

    g_hi = acc[7].astype(bf16)
    g_lo = (acc[7] - g_hi.astype(f32)).astype(bf16)
    whole(31, ag_s.at[0]).wait()
    whole(31, cc_s.at[0]).wait()
    for o in (1, 2, 3):
        @pl.when(x - o >= 0)
        def _():
            kvs[o].wait_recv()

    row = lax.broadcasted_iota(jnp.int32, (64, 256), 0)
    col = lax.broadcasted_iota(jnp.int32, (64, 256), 1)
    allowed = col <= row + x * 64
    mixed = [[], []]
    for b in range(2):
        s = dot_general(q[b * 64 : b * 64 + 64], kv[0, b], 1, 1) / math.sqrt(128.0)
        s = jnp.where(allowed, s, -1e30)
        e = jnp.exp(s - jnp.max(s, axis=1, keepdims=True))
        e = jnp.where(allowed, e, 0.0)
        w = (e / jnp.sum(e, axis=1, keepdims=True)).astype(bf16)
        att[b] = w
        for m in range(2):
            mixed[m].append(dot(w, kv[1 + m, b]).astype(bf16))

    xx, xt, po, to = stat[0][:, 0:1], stat[1][:, 0:1], acc[5], acc[6]
    logits, invs, projs = [], [], []
    for m in range(2):
        mix = jnp.concatenate(mixed[m], axis=0)
        mg = dot(mix, g_hi) + dot(mix, g_lo)
        mixf = mix.astype(f32)
        sq = xx + jnp.sum(mixf * (2.0 * po + mg), axis=1, keepdims=True)
        inv = lax.rsqrt(sq / 8192.0 + eps_norm)
        logits.append(inv * (xt + jnp.sum(mixf * to, axis=1, keepdims=True)))
        invs.append(inv)
        projs.append(po + mg)
    token = lax.broadcasted_iota(jnp.int32, (128, 1), 0)
    start = jnp.where(token < 64, 256 - rlen[0], 256 - rlen[1])
    sign = jnp.where(token < 64, 1.0, -1.0)
    resp = jnp.where(x * 64 + token % 64 >= start, sign, 0.0)
    part = jnp.sum(resp * (logits[1] - logits[0]), axis=0, keepdims=True)

    mgs[...] = jnp.broadcast_to(part, (8, 128))
    mgc = [remote(mgs, mgr.at[o], mg_s.at[o], mg_r.at[o], dev((x + o) % 4, y, z, c)) for o in range(4)]
    for o in (1, 2, 3):
        mgc[o].start()

    head = (resp * invs[1] * (to - (logits[1] / 8192.0) * invs[1] * projs[1])).astype(bf16)
    for b in range(2):
        terms = dot_general(att[b], head[b * 64 : b * 64 + 64], 0, 0)
        vgs[b] = terms.astype(bf16)
        vgo[b] = terms
    vgc = []
    for o in range(4):
        target = (x + 4 - o) % 4
        src = vgs.at[:, pl.ds(pl.multiple_of(target * 64, 64), 64), :]
        vgc.append(remote(src, vgr.at[o], vg_s.at[o], vg_r.at[o], dev(target, y, z, c)))
    for o in (1, 2, 3):
        @pl.when(x - o >= 0)
        def _():
            vgc[o].start()
    for o in (1, 2, 3):
        mgc[o].wait()
    margin = beta_dpo * (mgs[...] + mgr[1] + mgr[2] + mgr[3])
    pull = (-beta_dpo / 128.0) / (1.0 + jnp.exp(margin))
    loss = jnp.maximum(-margin, 0.0) + jnp.log1p(jnp.exp(-jnp.abs(margin)))
    mine = [vgo[b, own, :] for b in range(2)]
    total = jnp.concatenate(mine, axis=0)
    vgo[0, 0:128, :] = total
    for o in (1, 2, 3):
        @pl.when(x + o < 4)
        def _():
            vgc[o].wait_recv()
            vgo[0, 0:128, :] += vgr[o].reshape(128, 128).astype(f32)
    vg = (vgo[0, 0:128, :] * pull[0:1, :]).astype(bf16)

    up = dot_general(d_in, vg, 0, 0)
    agt = dot_general(aup[...], vg, 1, 1).astype(bf16)

    us[...] = up
    keep = pl.ds(pl.multiple_of(c * 32, 32), 32)
    give = pl.ds(pl.multiple_of(32 - c * 32, 32), 32)
    ucs[32:40, :] = loss
    ucs[0:32, :] = us[give, :]
    uc = remote(ucs, ucr, uc_s.at[0], uc_r.at[0], sib)
    uc.start()

    ag_both = jnp.where(c == 0, jnp.concatenate([agt[32:64], agt[0:32]], axis=0), agt)
    dcs = []
    for n in range(4):
        for i in range(2):
            g = n * 8 + i * 4
            both = dot(ag_both, nx[:, g * 256 : g * 256 + 1024])
            for k in range(4):
                dsend[g + k] = both[0:32, k * 256 : k * 256 + 256].astype(bf16)
                dkeep[g + k] = both[32:64, k * 256 : k * 256 + 256]
        cp = remote(dsend.at[pl.ds(n * 8, 8)], drecv.at[pl.ds(n * 8, 8)], dc_s.at[n], dc_r.at[n], sib)
        cp.start()
        dcs.append(cp)

    uc.wait()
    uxs[0:32, :] = us[keep, :] + ucr[0:32, :]
    uxs[32:40, :] = loss + ucr[32:40, :]
    uxc = [remote(uxs, uxr.at[o], ux_s.at[o], ux_r.at[o], dev((x + o) % 4, y, z, c)) for o in range(4)]
    for o in (1, 2, 3):
        uxc[o].start()

    for n in range(4):
        dcs[n].wait_recv()
        s1[n] = (dkeep[n * 8 : n * 8 + 8] + drecv[n * 8 : n * 8 + 8].astype(f32)).astype(bf16)

    y1, z1 = [], []
    for o in range(8):
        ty, tz = (y + o) % 8, (z + o) % 8
        y1.append(remote(s1.at[:, ty, pl.ds(0, 16), :], r1y.at[o], y1_s.at[o], y1_r.at[o], dev(x, ty, z, c)))
        z1.append(remote(s1.at[tz // 2, pl.ds((tz % 2) * 4, 4), pl.ds(16, 16), :], r1z.at[o], z1_s.at[o], z1_r.at[o],
                         dev(x, y, tz, c)))
    for o in (4, 3, 5, 2, 6, 1, 7):
        y1[o].start()
        z1[o].start()
    for o in (1, 2, 3):
        uxc[o].wait()
    uys[...] = uxs[...] + uxr[1] + uxr[2] + uxr[3]
    uyc = [remote(uys, uyr.at[o], uy_s.at[o], uy_r.at[o], dev(x, (y + o) % 8, z, c)) for o in range(8)]
    for o in range(1, 8):
        uyc[o].start()
    for o in range(1, 8):
        y1[o].wait()
        z1[o].wait()
    sy = s1[:, y, 0:16, :].astype(f32)
    sz = s1[h, pl.ds(zl * 4, 4), 16:32, :].astype(f32)
    for o in range(1, 8):
        sy += r1y[o].astype(f32)
        sz += r1z[o].astype(f32)
    s2y[...] = sy.astype(bf16)
    s2z[...] = sz.astype(bf16)

    y2 = []
    for o in range(8):
        tz = (z + o) % 8
        y2.append(remote(s2y.at[tz // 2], r2y.at[o], y2_s.at[o], y2_r.at[o], dev(x, y, tz, c)))
    for o in range(1, 8):
        y2[o].start()
    z2 = []
    for j in range(4):
        for zz in range(2):
            ty = zl * 4 + j
            z2.append((remote(s2z.at[j], r2z.at[y], z2_s.at[j * 2 + zz], z2_r.at[y], dev(x, ty, h * 2 + zz, c)),
                       jnp.logical_and(ty == y, zz == zl), j))
    for cp, me, j in z2:
        @pl.when(jnp.logical_not(me))
        def _():
            cp.start()
        @pl.when(me)
        def _():
            r2z[y] = s2z[j]
    for o in range(1, 8):
        uyc[o].wait()
    tot = uys[...]
    for o in range(1, 8):
        tot += uyr[o]
    uzs[...] = tot
    uzc = [remote(uzs, uzr.at[o], uz_s.at[o], uz_r.at[o], dev(x, y, (z + o) % 8, c)) for o in range(8)]
    for o in range(1, 8):
        uzc[o].start()
    for o in range(1, 8):
        y2[o].wait()
    for cp, me, j in z2:
        @pl.when(jnp.logical_not(me))
        def _():
            cp.wait_send()
    for s in range(8):
        @pl.when(jnp.logical_not(jnp.logical_and(s == y, y // 4 == zl)))
        def _():
            remote(s2z.at[0], r2z.at[s], z2_s.at[0], z2_r.at[s], sib).wait_recv()
    ty_ = s2y[h].astype(f32)
    tz_ = r2z[0].astype(f32)
    for o in range(1, 8):
        ty_ += r2y[o].astype(f32)
        tz_ += r2z[o].astype(f32)
    for k in range(2):
        s3[k, 0:16, :] = ty_[:, k * 128 : k * 128 + 128]
        s3[k, 16:32, :] = tz_[:, k * 128 : k * 128 + 128]

    x3 = []
    for o in range(4):
        tx = (x + o) % 4
        x3.append(remote(s3.at[tx // 2], r3.at[o], x3_s.at[o], x3_r.at[o], dev(tx, y, z, c)))
    for o in (1, 2, 3):
        x3[o].start()
    for o in range(1, 8):
        uzc[o].wait()
    tot = uzs[...]
    for o in range(1, 8):
        tot += uzr[o]
    ues[...] = tot[0:32, :]
    ue = remote(ues, uer, ue_s.at[0], ue_r.at[0], sib)
    ue.start()
    out_ref[128:136, :] = tot[32:40, :] * (1.0 / 512.0)
    for o in (1, 2, 3):
        x3[o].wait()
    mine = s3[x // 2] + r3[1] + r3[2] + r3[3]
    s4[...] = mine
    c4 = remote(s4, r4, c4_s.at[0], c4_r.at[0], sib)
    c4.start()
    ue.wait()
    out_ref[keep, :] = ues[...]
    out_ref[give, :] = uer[...]
    for o in (1, 2, 3):
        @pl.when(x + o < 4)
        def _():
            kvs[o].wait_send()
        @pl.when(x - o >= 0)
        def _():
            vgc[o].wait_send()
    for n in range(4):
        dcs[n].wait_send()
    c4.wait()
    low = jnp.where(c == 0, s4[...], r4[...])
    high = jnp.where(c == 0, r4[...], s4[...])
    whole = jnp.concatenate([low, high], axis=0)
    whole = jnp.where(x % 2 == 0, whole, pltpu.roll(whole, 64, 1))
    out_ref[64:128, 0:64] = whole.T[0:64, :]
    out_ref[64:128, 64:128] = jnp.zeros((64, 64), f32)

def split(packed, loss_ref, gdown_ref, gup_ref):
    loss_ref[0, 0] = jnp.max(packed[128:136, :])
    gdown_ref[...] = packed[64:128, 0:64]
    gup_ref[...] = packed[0:64, :]

def step(x_in, t_in, rlen, scale, wq, wk, wv, wo, wd, aup):
    f32, bf16 = jnp.float32, jnp.bfloat16
    V = pltpu.VMEM
    D = pltpu.SemaphoreType.DMA
    vm = pl.BlockSpec(memory_space=pltpu.VMEM)
    hb = pl.BlockSpec(memory_space=pl.ANY)
    packed = pl.pallas_call(
        kernel,
        name="dpo_step",
        out_shape=jax.ShapeDtypeStruct((136, 128), f32),
        in_specs=[hb, hb, pl.BlockSpec(memory_space=pltpu.SMEM)] + [vm] * 7,
        out_specs=vm,
        scratch_shapes=[
            V((128, 8192), bf16), V((128, 8192), bf16), V((128, 8192), bf16),
            V((32, 1152, 128), bf16), V((8, 128, 128), f32), V((3, 2, 256, 128), bf16), V((2, 64, 256), bf16),
            V((2, 256, 128), bf16), V((4, 2, 64, 128), bf16), V((2, 256, 128), f32), V((8, 128), f32), V((4, 8, 128), f32),
            V((32, 32, 256), f32), V((32, 32, 256), bf16), V((32, 32, 256), bf16), V((4, 8, 32, 256), bf16),
            V((8, 4, 16, 256), bf16), V((8, 4, 16, 256), bf16), V((4, 16, 256), bf16), V((4, 16, 256), bf16),
            V((8, 16, 256), bf16), V((8, 16, 256), bf16), V((2, 32, 128), f32), V((4, 32, 128), f32),
            V((32, 128), f32), V((32, 128), f32),
            V((64, 128), f32), V((64, 128), f32), V((40, 128), f32), V((4, 40, 128), f32), V((40, 128), f32),
            V((8, 40, 128), f32), V((40, 128), f32), V((8, 40, 128), f32), V((40, 128), f32), V((40, 128), f32), V((32, 128), f32), V((32, 128), f32),
            V((4, 128, 128), f32),
            D((2,)), D((1,)), D((SENDS,)), D((1,)), D((8,)), D((4,)), D((4,)), D((4,)), D((4,)), D((4,)), D((4,)),
            D((4,)), D((4,)), D((8,)), D((8,)), D((8,)), D((8,)), D((8,)), D((8,)), D((8,)), D((8,)), D((4,)), D((4,)),
            D((1,)), D((1,)), D((1,)), D((1,)), D((4,)), D((4,)), D((8,)), D((8,)), D((8,)), D((8,)), D((1,)), D((1,)),
        ],
        compiler_params=pltpu.CompilerParams(
            collective_id=0, has_side_effects=True, vmem_limit_bytes=56 * 2**20
        ),
    )(
        x_in.reshape(128, 8192), t_in.reshape(128, 8192), rlen, scale.reshape(1, 8192), wq, wk, wv, wo, wd.T, aup
    )
    loss, gdown, gup = pl.pallas_call(
        split,
        name="split",
        out_shape=(
            jax.ShapeDtypeStruct((1, 1), f32),
            jax.ShapeDtypeStruct((64, 64), f32),
            jax.ShapeDtypeStruct((64, 128), f32),
        ),
        in_specs=[vm],
        out_specs=(pl.BlockSpec(memory_space=pltpu.SMEM), vm, vm),
    )(packed)
    return loss.reshape(()), gdown, gup

def solution(mesh):
    return jax.shard_map(
        step,
        mesh=mesh,
        in_specs=(
            P(("dp", "fsdp"), "seq", None),
            P(("dp", "fsdp"), "seq", None),
            P(("dp", "fsdp")),
            P(),
            P("fsdp", None),
            P("fsdp", None),
            P("fsdp", None),
            P("fsdp", None),
            P("fsdp", None),
            P(),
        ),
        out_specs=(P(), P(("fsdp", "seq"), None), P()),
        check_vma=False,
    )
```

```python
import math

import jax
import jax.numpy as jnp
from jax import lax
from jax.experimental import pallas as pl
from jax.experimental.pallas import tpu as pltpu
from jax.sharding import PartitionSpec as P

theta_base = 500000.0
beta_dpo = 0.1
eps_norm = 1e-05

PARTS = 2
SENDS = 124
GATHER = (
    (0,4,0,0,1,0), (0,3,0,0,0,0), (0,2,0,0,1,1), (0,2,0,0,0,0), (0,3,0,0,0,1), (0,4,0,0,0,1), (0,3,0,0,1,0),
    (0,4,0,0,1,1), (0,2,0,0,0,1), (2,), (0,3,0,0,1,1), (0,2,0,0,1,0), (0,4,0,0,0,0), (1,0), (0,5,0,1,1,0), (1,2),
    (0,2,7,0,1,1), (1,1), (0,3,1,0,0,0), (0,4,1,0,0,0), (1,5), (0,5,0,1,0,1), (1,4), (0,3,1,0,0,1), (0,4,7,0,1,1),
    (1,3), (0,2,7,0,0,0), (1,7), (0,5,0,1,1,1), (0,2,0,1,1,0), (0,4,1,0,0,1), (1,6), (0,3,1,0,1,0), (1,11),
    (0,5,0,1,0,0), (1,9), (0,3,1,0,1,1), (1,10), (0,2,7,0,1,0), (1,8), (0,4,7,0,0,1), (1,15), (0,5,1,1,0,0), (1,13),
    (0,0,6,0,1,1), (0,1,1,1,0,0), (0,2,6,0,1,1), (1,14), (0,3,2,0,0,0), (1,12), (0,4,0,2,1,0), (1,18), (0,5,7,1,1,1),
    (1,19), (0,2,6,0,0,0), (1,17), (0,3,2,0,0,1), (1,16), (0,4,0,2,0,1), (1,21), (0,5,7,1,1,0), (3,0,1,4,28), (1,22),
    (0,1,1,1,0,1), (0,0,7,1,1,0), (0,2,7,1,1,0), (1,23), (0,4,2,0,1,0), (1,20), (0,3,0,2,1,1), (1,27), (0,5,7,1,0,1),
    (0,2,7,1,0,1), (0,3,1,1,0,1), (0,4,0,2,1,1), (1,28), (0,0,1,2,0,0), (0,5,1,1,0,1), (1,33), (0,1,0,3,1,0),
    (0,2,0,3,1,0), (0,3,1,2,0,0), (0,4,1,2,0,0), (1,24), (1,25), (1,26), (1,31), (0,0,5,0,1,1), (1,36),
    (0,1,3,0,0,1), (1,37), (0,3,0,3,0,1), (1,34), (0,2,7,2,1,1), (0,4,7,2,1,1), (1,29), (1,30), (1,32), (1,40),
    (0,5,7,1,0,0), (1,35), (0,0,5,0,0,0), (0,1,3,0,0,0), (1,41), (0,2,6,1,1,0), (1,43), (0,3,1,2,1,1), (0,4,3,0,0,0),
    (0,5,6,1,1,0), (0,0,6,1,1,0), (1,46), (0,1,2,1,0,1), (0,2,5,0,1,1), (0,4,5,0,1,1), (0,3,0,3,1,0), (1,38), (1,39),
    (1,42), (1,45), (0,0,6,1,0,1), (0,5,6,1,0,1), (1,51), (0,1,7,3,1,0), (0,2,7,3,1,0), (0,4,3,0,0,1), (1,52),
    (0,3,2,2,0,0), (1,44), (1,47), (0,0,2,2,0,0), (3,2,8,24,29), (0,5,2,1,0,1), (1,56), (0,1,1,3,0,1), (0,3,1,3,0,1),
    (1,58), (0,2,7,3,1,1), (0,4,2,2,0,0), (1,48), (1,49), (1,50), (1,53), (0,5,2,2,0,0), (0,0,7,3,1,1), (1,62),
    (0,1,5,1,1,0), (1,55), (0,4,3,0,1,1), (1,63), (0,3,2,2,1,1), (0,2,5,1,1,0), (1,54), (1,57), (1,65),
    (0,0,6,2,1,0), (0,5,5,1,1,0), (1,68), (0,1,4,0,1,1), (0,4,2,2,1,1), (0,2,6,2,1,1), (0,3,3,0,0,0), (1,59), (1,60),
    (1,61), (1,64), (1,69), (0,0,5,1,1,1), (1,75), (0,5,3,1,0,1), (1,76), (0,1,3,2,0,0), (0,4,3,2,0,0), (1,74),
    (0,2,6,3,1,0), (0,3,3,2,0,0), (1,66), (1,67), (1,70), (0,0,6,3,1,0), (1,81), (0,1,6,3,1,1), (0,4,4,0,1,1),
    (0,2,6,3,1,1), (1,80), (0,3,2,3,0,1), (1,71), (1,72), (1,73), (1,85), (0,5,5,1,0,0), (1,82), (0,0,2,3,0,0),
    (1,88), (0,1,4,1,1,0), (1,87), (0,4,3,2,1,1), (0,2,6,2,0,1), (0,3,3,2,1,1), (1,77), (1,78), (1,79),
    (0,5,4,1,1,0), (3,3,5,6,12,20,30), (0,0,3,1,0,0), (1,94), (0,1,4,0,0,0), (1,91), (0,4,4,0,0,1), (1,83), (1,84),
    (1,86), (1,96), (0,3,3,2,0,1), (1,99), (0,2,5,3,1,0), (0,0,5,3,1,0), (1,98), (0,1,3,3,0,0), (1,100),
    (0,4,4,2,0,0), (1,89), (1,90), (1,92), (1,93), (1,105), (0,3,3,3,0,1), (1,104), (0,0,5,3,1,1), (0,2,5,3,1,1),
    (1,95), (1,97), (1,101), (1,102), (1,103), (1,106), (1,107), (1,108), (1,109), (1,110), (1,111), (1,112),
    (3,7,9,10,14,21,25,31), (1,113), (1,114), (1,115), (1,116), (1,117), (1,118), (1,119), (1,120), (1,121),
    (3,11,22,26,27), (1,122), (1,123), (3,13,15,16,17,18,19,23),
)

def arrives(way, piece):
    dy, pair, half, part = piece
    if way < 2:
        return (dy, pair, 1 - half, part)
    if way == 2:
        return ((dy - 1) % 8, pair, half, part)
    if way == 3:
        return ((dy + 1) % 8, pair, half, part)
    if way == 4:
        return (dy, (1, 0, 3, 2)[pair], half, part)
    return (dy, (0, 2, 1, 3)[pair], half, part)

def dot(a, b):
    return jnp.dot(a, b, preferred_element_type=jnp.float32)

def dot_general(a, b, ca, cb):
    return lax.dot_general(a, b, (((ca,), (cb,)), ((), ())), preferred_element_type=jnp.float32)

def kernel(
    x_hbm, t_hbm, rlen, scale_hbm, wq, wk, wv, wo, wd, aup_hbm,
    out_ref,
    xs, ts, scale, aup, nx, W, acc, kv, att, vgs, vgr, vgo, mgs, mgr,
    dkeep, dsend, drecv, s1, r1y, r1z, s2y, s2z, r2y, r2z, s3, r3, s4, r4,
    us, uxs, uxr, uys, uyr, uzs, uzr, ucs, ucr, uas, uer, stat,
    in_sem, ag_s, ag_r, cc_s, cc_r, kv_s, kv_r, vg_s, vg_r, mg_s, mg_r, dc_s, dc_r,
    y1_s, y1_r, z1_s, z1_r, y2_s, y2_r, z2_s, z2_r, x3_s, x3_r, c4_s, c4_r,
    uc_s, uc_r, ux_s, ux_r, uy_s, uy_r, uz_s, uz_r, ue_s, ue_r, ua_s, ua_r,
):
    f32, bf16 = jnp.float32, jnp.bfloat16
    dp, f, x = lax.axis_index("dp"), lax.axis_index("fsdp"), lax.axis_index("seq")
    h, y, zl, c = f // 8, f % 8, dp // 2, dp % 2
    z = h * 2 + zl

    def dev(xx, yy, zz, cc):
        return {"dp": (zz % 2) * 2 + cc, "fsdp": (zz // 2) * 8 + yy, "seq": xx}

    outer = (z + 7 + 2 * zl) % 8
    inner = (z + 1 + 6 * zl) % 8
    sib = dev(x, y, z, 1 - c)
    ways = [
        dev((x + 1) % 4, y, z, c),
        dev((x + 3) % 4, y, z, c),
        dev(x, (y + 1) % 8, z, c),
        dev(x, (y + 7) % 8, z, c),
        dev(x, y, outer, c),
        dev(x, y, inner, c),
    ]

    def remote(src, dst, ss, rs, to):
        return pltpu.make_async_remote_copy(src_ref=src, dst_ref=dst, send_sem=ss, recv_sem=rs, device_id=to)

    in_x = pltpu.make_async_copy(x_hbm, xs, in_sem.at[0])
    in_t = pltpu.make_async_copy(t_hbm, ts, in_sem.at[1])

    own_in = [
        pltpu.make_async_copy(w, W.at[f, pl.ds(k * 288, 256), :], in_sem.at[2 + k])
        for k, w in enumerate((wq, wk, wv, wo))
    ]
    own_in += [
        pltpu.make_async_copy(
            wd.at[pl.ds((k % 2) * 32, 32), pl.ds((k // 2) * 128, 128)],
            W.at[f, pl.ds(k * 288 + 256, 32), :],
            in_sem.at[6 + k],
        )
        for k in range(4)
    ]
    in_scale = pltpu.make_async_copy(scale_hbm, scale, in_sem.at[10])
    in_aup = pltpu.make_async_copy(aup_hbm, aup, in_sem.at[11])
    for cp in own_in + [in_scale, in_aup]:
        cp.start()
    in_x.start()
    in_t.start()
    kv[...] = jnp.zeros_like(kv)

    barrier = pltpu.get_barrier_semaphore()
    greet = [sib]
    greet += [dev((x + o) % 4, y, z, c) for o in (1, 2, 3)]
    greet += [dev(x, (y + o) % 8, z, c) for o in range(1, 8)]
    greet += [dev(x, y, (z + o) % 8, c) for o in range(1, 8)]
    other = z + 1 - 2 * zl
    greet += [dev(x, (y + o) % 8, other, c) for o in range(1, 8)]
    for to in greet:
        pl.semaphore_signal(barrier, inc=1, device_id=to)
    acc[...] = jnp.zeros_like(acc)
    for cp in own_in + [in_scale, in_aup]:
        cp.wait()
    pl.semaphore_wait(barrier, len(greet))

    pairs = [h, (h + 3 + 2 * zl) % 4, (h + 1 + 2 * (1 - zl) * 0 + 2 * zl) % 4, (h + 2) % 4]
    pairs[1] = (h + 3 + 2 * zl) % 4
    pairs[2] = (h + 1 + 2 * zl) % 4

    def region(piece):
        dy, pair, half, part = piece
        rows = (c * 2 + (half + x) % 2) * 288 + part * (288 // PARTS)
        return W.at[pairs[pair] * 8 + (y + dy) % 8, pl.ds(pl.multiple_of(rows, 16), 288 // PARTS), :]

    groups = [do[1:] for do in GATHER if do[0] == 3]
    group_of = {block: k for k, blocks in enumerate(groups) for block in blocks}
    sends, came = [], []
    for do in GATHER:
        if do[0] == 0:
            n = len(sends)
            a = region(do[2:])
            came.append(arrives(do[1], do[2:]))
            sends.append(remote(a, a, ag_s.at[0], ag_r.at[n], ways[do[1]]))

    def half_block(dy, pair, half):
        rows = (c * 2 + (half + x) % 2) * 288
        return W.at[pairs[pair] * 8 + (y + dy) % 8, pl.ds(pl.multiple_of(rows, 16), 288), :]

    def whole(blocks, sem):
        ref = W.at[pl.ds(0, blocks), pl.ds(0, 576), :]
        return pltpu.make_async_copy(ref, ref, sem)

    parts_in = {}

    def arrive(n):
        dy, pair, half, _ = came[n]
        sends[n].wait_recv()
        parts_in[dy, pair, half] = parts_in.get((dy, pair, half), 0) + 1
        if parts_in[dy, pair, half] == PARTS:
            a = half_block(dy, pair, half)
            remote(a, a, cc_s.at[0], cc_r.at[group_of[dy * 4 + pair]], sib).start()

    def norm_rows():
        in_x.wait()
        in_t.wait()
        width = 1024

        def sums(i, carry):
            xx, xt = carry
            cols = pl.ds(pl.multiple_of(i * width, width), width)
            a = xs[:, cols].astype(f32)
            b = ts[:, cols].astype(f32)
            return xx + jnp.sum(a * a, axis=1, keepdims=True), xt + jnp.sum(a * b, axis=1, keepdims=True)

        zero = jnp.zeros((128, 1), f32)
        xx, xt = lax.fori_loop(0, 8192 // width, sums, (zero, zero))
        stat[0] = jnp.broadcast_to(xx, (128, 128))
        stat[1] = jnp.broadcast_to(xt, (128, 128))
        inv = lax.rsqrt(xx / 8192.0 + eps_norm)

        def rows(i, carry):
            cols = pl.ds(pl.multiple_of(i * width, width), width)
            nx[:, cols] = (xs[:, cols].astype(f32) * inv * scale[:, cols]).astype(bf16)
            return carry

        lax.fori_loop(0, 8192 // width, rows, 0)
        lane = lax.broadcasted_iota(jnp.int32, (128, 128), 1)
        token = lax.broadcasted_iota(jnp.int32, (128, 128), 0)
        position = (x * 64 + token % 64).astype(f32)
        rate = jnp.exp((lane % 64).astype(f32) * (-2.0 / 128.0 * math.log(theta_base)))
        angle = position * rate
        stat[2] = jnp.cos(angle)
        sine = jnp.sin(angle)
        stat[3] = jnp.where(lane < 64, -sine, sine)

    def multiply(blocks):
        whole(len(blocks) - (0 in blocks), cc_r.at[group_of[blocks[0]]]).wait()

        def body(i, carry):
            g = jnp.int32(0)
            for k, block in enumerate(blocks):
                g += jnp.where(i == k, 1, 0) * (pairs[block % 4] * 8 + (y + block // 4) % 8)
            cols = pl.ds(pl.multiple_of(g * 256, 256), 256)
            a, raw, tgt = nx[:, cols], xs[:, cols], ts[:, cols]
            qk = jnp.concatenate([W[g, 0:256, :], W[g, 288:544, :]], axis=1)
            out = W[g, 864:1120, :]
            down = jnp.concatenate(
                [jnp.concatenate([W[g, 288 * k + 256 : 288 * k + 288, :] for k in (k0, k0 + 1)], axis=0) for k0 in (0, 2)],
                axis=1,
            )
            both = dot(a, qk)
            acc[0] += both[:, 0:128]
            acc[1] += both[:, 128:256]
            acc[2] += dot(a, W[g, 576:832, :])
            acc[3, :, 0:64] += dot_general(a, down, 1, 1)
            acc[5] += dot(raw, out)
            acc[6] += dot(tgt, out)
            acc[7] += dot_general(out, out, 0, 0)
            return carry

        lax.fori_loop(0, len(blocks), body, 0, unroll=2)

    n = 0
    for do in GATHER:
        if do[0] == 0:
            sends[n].start()
            n += 1
        elif do[0] == 1:
            arrive(do[1])
        elif do[0] == 2:
            norm_rows()
        else:
            multiply(do[1:])

    def rope(v):
        return (v * stat[2] + pltpu.roll(v, 64, 1) * stat[3]).astype(bf16)

    q = rope(acc[0])
    own = pl.ds(pl.multiple_of(x * 64, 64), 64)
    d_in = acc[3, :, 0:64].astype(bf16)
    base = acc[2]
    k_own = rope(acc[1])
    v_ref = base.astype(bf16)
    v_pol = (base + dot(d_in, aup[...])).astype(bf16)
    for b in range(2):
        kv[0, b, own, :] = k_own[b * 64 : b * 64 + 64]
        kv[1, b, own, :] = v_ref[b * 64 : b * 64 + 64]
        kv[2, b, own, :] = v_pol[b * 64 : b * 64 + 64]
    kv_own = kv.at[:, :, own, :]
    kvs = [remote(kv_own, kv_own, kv_s.at[o], kv_r.at[o], dev((x + o) % 4, y, z, c)) for o in range(4)]
    for o in (1, 2, 3):
        @pl.when(x + o < 4)
        def _():
            kvs[o].start()

    def waitkv():
        for o in (1, 2, 3):
            @pl.when(x + o < 4)
            def _():
                kvs[o].wait_send()

    def waitvg():
        for o in (1, 2, 3):
            @pl.when(x - o >= 0)
            def _():
                vgc[o].wait_send()

    g_hi = acc[7].astype(bf16)
    g_lo = (acc[7] - g_hi.astype(f32)).astype(bf16)
    whole(31, ag_s.at[0]).wait()
    whole(31, cc_s.at[0]).wait()
    for o in (1, 2, 3):
        @pl.when(x - o >= 0)
        def _():
            kvs[o].wait_recv()

    row = lax.broadcasted_iota(jnp.int32, (64, 256), 0)
    col = lax.broadcasted_iota(jnp.int32, (64, 256), 1)
    allowed = col <= row + x * 64
    mixed = [[], []]
    for b in range(2):
        s = dot_general(q[b * 64 : b * 64 + 64], kv[0, b], 1, 1) / math.sqrt(128.0)
        s = jnp.where(allowed, s, -1e30)
        e = jnp.exp(s - jnp.max(s, axis=1, keepdims=True))
        e = jnp.where(allowed, e, 0.0)
        w = (e / jnp.sum(e, axis=1, keepdims=True)).astype(bf16)
        att[b] = w
        for m in range(2):
            mixed[m].append(dot(w, kv[1 + m, b]).astype(bf16))

    xx, xt, po, to = stat[0][:, 0:1], stat[1][:, 0:1], acc[5], acc[6]
    logits, invs, projs = [], [], []
    for m in range(2):
        mix = jnp.concatenate(mixed[m], axis=0)
        mg = dot(mix, g_hi) + dot(mix, g_lo)
        mixf = mix.astype(f32)
        sq = xx + jnp.sum(mixf * (2.0 * po + mg), axis=1, keepdims=True)
        inv = lax.rsqrt(sq / 8192.0 + eps_norm)
        logits.append(inv * (xt + jnp.sum(mixf * to, axis=1, keepdims=True)))
        invs.append(inv)
        projs.append(po + mg)
    token = lax.broadcasted_iota(jnp.int32, (128, 1), 0)
    start = jnp.where(token < 64, 256 - rlen[0], 256 - rlen[1])
    sign = jnp.where(token < 64, 1.0, -1.0)
    resp = jnp.where(x * 64 + token % 64 >= start, sign, 0.0)
    part = jnp.sum(resp * (logits[1] - logits[0]), axis=0, keepdims=True)

    mgs[...] = jnp.broadcast_to(part, (8, 128))
    mgc = [remote(mgs, mgr.at[o], mg_s.at[o], mg_r.at[o], dev((x + o) % 4, y, z, c)) for o in range(4)]
    for o in (1, 2, 3):
        mgc[o].start()

    head = (resp * invs[1] * (to - (logits[1] / 8192.0) * invs[1] * projs[1])).astype(bf16)
    for b in range(2):
        terms = dot_general(att[b], head[b * 64 : b * 64 + 64], 0, 0)
        vgs[b] = terms.astype(bf16)
        vgo[b] = terms
    vgc = []
    for o in range(4):
        target = (x + 4 - o) % 4
        src = vgs.at[:, pl.ds(pl.multiple_of(target * 64, 64), 64), :]
        vgc.append(remote(src, vgr.at[o], vg_s.at[o], vg_r.at[o], dev(target, y, z, c)))
    for o in (1, 2, 3):
        @pl.when(x - o >= 0)
        def _():
            vgc[o].start()
    for o in (1, 2, 3):
        mgc[o].wait()
    margin = beta_dpo * (mgs[...] + mgr[1] + mgr[2] + mgr[3])
    pull = (-beta_dpo / 128.0) / (1.0 + jnp.exp(margin))
    loss = jnp.maximum(-margin, 0.0) + jnp.log1p(jnp.exp(-jnp.abs(margin)))
    mine = [vgo[b, own, :] for b in range(2)]
    total = jnp.concatenate(mine, axis=0)
    vgo[0, 0:128, :] = total
    for o in (1, 2, 3):
        @pl.when(x + o < 4)
        def _():
            vgc[o].wait_recv()
            vgo[0, 0:128, :] += vgr[o].reshape(128, 128).astype(f32)
    vg = (vgo[0, 0:128, :] * pull[0:1, :]).astype(bf16)

    up = dot_general(d_in, vg, 0, 0)
    agt = dot_general(aup[...], vg, 1, 1).astype(bf16)

    us[...] = up
    keep = pl.ds(pl.multiple_of(c * 32, 32), 32)
    give = pl.ds(pl.multiple_of(32 - c * 32, 32), 32)
    ucs[32:40, :] = loss
    ucs[0:32, :] = us[give, :]
    uc = remote(ucs, ucr, uc_s.at[0], uc_r.at[0], sib)
    uc.start()

    ag_both = jnp.where(c == 0, jnp.concatenate([agt[32:64], agt[0:32]], axis=0), agt)
    dcs = []
    for n in range(4):
        for i in range(2):
            g = n * 8 + i * 4
            both = dot(ag_both, nx[:, g * 256 : g * 256 + 1024])
            for k in range(4):
                dsend[g + k] = both[0:32, k * 256 : k * 256 + 256].astype(bf16)
                dkeep[g + k] = both[32:64, k * 256 : k * 256 + 256]
        cp = remote(dsend.at[pl.ds(n * 8, 8)], drecv.at[pl.ds(n * 8, 8)], dc_s.at[n], dc_r.at[n], sib)
        cp.start()
        dcs.append(cp)

    uc.wait()
    uxs[...] = us[keep, :] + ucr[0:32, :]
    uys[8:16, :] = loss + ucr[32:40, :]
    uxc = []
    for o in range(4):
        tx = (x + o) % 4
        src = uxs.at[pl.ds(pl.multiple_of(tx * 8, 8), 8), :]
        uxc.append(remote(src, uxr.at[o], ux_s.at[o], ux_r.at[o], dev(tx, y, z, c)))
    for o in (1, 2, 3):
        uxc[o].start()

    for n in range(4):
        dcs[n].wait_recv()
        s1[n] = (dkeep[n * 8 : n * 8 + 8] + drecv[n * 8 : n * 8 + 8].astype(f32)).astype(bf16)

    y1, z1 = [], []
    for o in range(8):
        ty, tz = (y + o) % 8, (z + o) % 8
        y1.append(remote(s1.at[:, ty, pl.ds(0, 16), :], r1y.at[o], y1_s.at[o], y1_r.at[o], dev(x, ty, z, c)))
        z1.append(remote(s1.at[tz // 2, pl.ds((tz % 2) * 4, 4), pl.ds(16, 16), :], r1z.at[o], z1_s.at[o], z1_r.at[o],
                         dev(x, y, tz, c)))
    for o in (4, 3, 5, 2, 6, 1, 7):
        y1[o].start()
        z1[o].start()
    for o in (1, 2, 3):
        uxc[o].wait()
    eighth = pl.ds(pl.multiple_of(x * 8, 8), 8)
    uys[0:8, :] = uxs[eighth, :] + uxr[1] + uxr[2] + uxr[3]
    uyc = [remote(uys, uyr.at[o], uy_s.at[o], uy_r.at[o], dev(x, (y + o) % 8, z, c)) for o in range(8)]
    for o in range(1, 8):
        uyc[o].start()
    for o in range(1, 8):
        y1[o].wait()
        z1[o].wait()
    sy = s1[:, y, 0:16, :].astype(f32)
    sz = s1[h, pl.ds(zl * 4, 4), 16:32, :].astype(f32)
    for o in range(1, 8):
        sy += r1y[o].astype(f32)
        sz += r1z[o].astype(f32)
    s2y[...] = sy.astype(bf16)
    s2z[...] = sz.astype(bf16)

    y2 = []
    for o in range(8):
        tz = (z + o) % 8
        y2.append(remote(s2y.at[tz // 2], r2y.at[o], y2_s.at[o], y2_r.at[o], dev(x, y, tz, c)))
    for o in range(1, 8):
        y2[o].start()
    z2 = []
    for j in range(4):
        for zz in range(2):
            ty = zl * 4 + j
            z2.append((remote(s2z.at[j], r2z.at[y], z2_s.at[j * 2 + zz], z2_r.at[y], dev(x, ty, h * 2 + zz, c)),
                       jnp.logical_and(ty == y, zz == zl), j))
    for cp, me, j in z2:
        @pl.when(jnp.logical_not(me))
        def _():
            cp.start()
        @pl.when(me)
        def _():
            r2z[y] = s2z[j]
    for o in range(1, 8):
        uyc[o].wait()
    tot = uys[...]
    for o in range(1, 8):
        tot += uyr[o]
    uzs[...] = tot
    uzc = [remote(uzs, uzr.at[o], uz_s.at[o], uz_r.at[o], dev(x, y, (z + o) % 8, c)) for o in range(8)]
    for o in range(1, 8):
        uzc[o].start()
    for o in range(1, 8):
        y2[o].wait()
    for cp, me, j in z2:
        @pl.when(jnp.logical_not(me))
        def _():
            cp.wait_send()
    for s in range(8):
        @pl.when(jnp.logical_not(jnp.logical_and(s == y, y // 4 == zl)))
        def _():
            remote(s2z.at[0], r2z.at[s], z2_s.at[0], z2_r.at[s], sib).wait_recv()
    ty_ = s2y[h].astype(f32)
    tz_ = r2z[0].astype(f32)
    for o in range(1, 8):
        ty_ += r2y[o].astype(f32)
        tz_ += r2z[o].astype(f32)
    for k in range(2):
        s3[k, 0:16, :] = ty_[:, k * 128 : k * 128 + 128]
        s3[k, 16:32, :] = tz_[:, k * 128 : k * 128 + 128]

    x3 = []
    for o in range(4):
        tx = (x + o) % 4
        x3.append(remote(s3.at[tx // 2], r3.at[o], x3_s.at[o], x3_r.at[o], dev(tx, y, z, c)))
    for o in (1, 2, 3):
        x3[o].start()
    for o in range(1, 8):
        uzc[o].wait()
    tot = uzs[...]
    for o in range(1, 8):
        tot += uzr[o]
    uas[eighth, :] = tot[0:8, :]
    uac = []
    for o in range(4):
        ref = uas.at[eighth, :]
        uac.append(remote(ref, ref, ua_s.at[o], ua_r.at[o], dev((x + o) % 4, y, z, c)))
    for o in (1, 2, 3):
        uac[o].start()
    out_ref[128:136, :] = tot[8:16, :] * (1.0 / 128.0)
    for o in (1, 2, 3):
        x3[o].wait()
    mine = s3[x // 2] + r3[1] + r3[2] + r3[3]
    s4[...] = mine
    c4 = remote(s4, r4, c4_s.at[0], c4_r.at[0], sib)
    c4.start()
    for o in (1, 2, 3):
        uac[o].wait()
    ue = remote(uas, uer, ue_s.at[0], ue_r.at[0], sib)
    ue.start()
    out_ref[keep, :] = uas[...]
    for o in (1, 2, 3):
        @pl.when(x + o < 4)
        def _():
            kvs[o].wait_send()
        @pl.when(x - o >= 0)
        def _():
            vgc[o].wait_send()
    for n in range(4):
        dcs[n].wait_send()
    c4.wait()
    ue.wait()
    out_ref[give, :] = uer[...]
    low = jnp.where(c == 0, s4[...], r4[...])
    high = jnp.where(c == 0, r4[...], s4[...])
    whole = jnp.concatenate([low, high], axis=0)
    whole = jnp.where(x % 2 == 0, whole, pltpu.roll(whole, 64, 1))
    out_ref[64:128, 0:64] = whole.T[0:64, :]
    out_ref[64:128, 64:128] = jnp.zeros((64, 64), f32)

def split(packed, loss_ref, gdown_ref, gup_ref):
    loss_ref[0, 0] = jnp.max(packed[128:136, :])
    gdown_ref[...] = packed[64:128, 0:64]
    gup_ref[...] = packed[0:64, :]

def step(x_in, t_in, rlen, scale, wq, wk, wv, wo, wd, aup):
    f32, bf16 = jnp.float32, jnp.bfloat16
    V = pltpu.VMEM
    D = pltpu.SemaphoreType.DMA
    vm = pl.BlockSpec(memory_space=pltpu.VMEM)
    hb = pl.BlockSpec(memory_space=pl.ANY)
    packed = pl.pallas_call(
        kernel,
        name="dpo_step",
        out_shape=jax.ShapeDtypeStruct((136, 128), f32),
        in_specs=[hb, hb, pl.BlockSpec(memory_space=pltpu.SMEM)] + [hb] * 7,
        out_specs=vm,
        scratch_shapes=[
            V((128, 8192), bf16), V((128, 8192), bf16), V((1, 8192), f32), V((64, 128), bf16), V((128, 8192), bf16),
            V((32, 1152, 128), bf16), V((8, 128, 128), f32), V((3, 2, 256, 128), bf16), V((2, 64, 256), bf16),
            V((2, 256, 128), bf16), V((4, 2, 64, 128), bf16), V((2, 256, 128), f32), V((8, 128), f32), V((4, 8, 128), f32),
            V((32, 32, 256), f32), V((32, 32, 256), bf16), V((32, 32, 256), bf16), V((4, 8, 32, 256), bf16),
            V((8, 4, 16, 256), bf16), V((8, 4, 16, 256), bf16), V((4, 16, 256), bf16), V((4, 16, 256), bf16),
            V((8, 16, 256), bf16), V((8, 16, 256), bf16), V((2, 32, 128), f32), V((4, 32, 128), f32),
            V((32, 128), f32), V((32, 128), f32),
            V((64, 128), f32), V((32, 128), f32), V((4, 8, 128), f32), V((16, 128), f32), V((8, 16, 128), f32),
            V((16, 128), f32), V((8, 16, 128), f32), V((40, 128), f32), V((40, 128), f32), V((32, 128), f32), V((32, 128), f32),
            V((4, 128, 128), f32),
            D((12,)), D((1,)), D((SENDS,)), D((1,)), D((8,)), D((4,)), D((4,)), D((4,)), D((4,)), D((4,)), D((4,)),
            D((4,)), D((4,)), D((8,)), D((8,)), D((8,)), D((8,)), D((8,)), D((8,)), D((8,)), D((8,)), D((4,)), D((4,)),
            D((1,)), D((1,)), D((1,)), D((1,)), D((4,)), D((4,)), D((8,)), D((8,)), D((8,)), D((8,)), D((1,)), D((1,)), D((4,)), D((4,)),
        ],
        compiler_params=pltpu.CompilerParams(
            collective_id=0, has_side_effects=True, vmem_limit_bytes=56 * 2**20
        ),
    )(
        x_in.reshape(128, 8192), t_in.reshape(128, 8192), rlen, scale.reshape(1, 8192), wq, wk, wv, wo, wd.T, aup
    )
    loss, gdown, gup = pl.pallas_call(
        split,
        name="split",
        out_shape=(
            jax.ShapeDtypeStruct((1, 1), f32),
            jax.ShapeDtypeStruct((64, 64), f32),
            jax.ShapeDtypeStruct((64, 128), f32),
        ),
        in_specs=[vm],
        out_specs=(pl.BlockSpec(memory_space=pltpu.SMEM), vm, vm),
    )(packed)
    return loss.reshape(()), gdown, gup

def solution(mesh):
    return jax.shard_map(
        step,
        mesh=mesh,
        in_specs=(
            P(("dp", "fsdp"), "seq", None),
            P(("dp", "fsdp"), "seq", None),
            P(("dp", "fsdp")),
            P(),
            P("fsdp", None),
            P("fsdp", None),
            P("fsdp", None),
            P("fsdp", None),
            P("fsdp", None),
            P(),
        ),
        out_specs=(P(), P(("fsdp", "seq"), None), P()),
        check_vma=False,
    )
```

```python
import math

import jax
import jax.numpy as jnp
from jax import lax
from jax.experimental import pallas as pl
from jax.experimental.pallas import tpu as pltpu
from jax.sharding import PartitionSpec as P

theta_base = 500000.0
beta_dpo = 0.1
eps_norm = 1e-05

PARTS = 2
SENDS = 124
GATHER = (
    (0,4,0,0,1,0), (0,3,0,0,0,0), (0,2,0,0,1,1), (0,2,0,0,0,0), (0,3,0,0,0,1), (0,4,0,0,0,1), (0,3,0,0,1,0),
    (0,4,0,0,1,1), (0,2,0,0,0,1), (2,), (0,3,0,0,1,1), (0,2,0,0,1,0), (0,4,0,0,0,0), (1,0), (0,5,0,1,1,0), (1,2),
    (0,2,7,0,1,1), (1,1), (0,3,1,0,0,0), (0,4,1,0,0,0), (1,5), (0,5,0,1,0,1), (1,4), (0,3,1,0,0,1), (0,4,7,0,1,1),
    (1,3), (0,2,7,0,0,0), (1,7), (0,5,0,1,1,1), (0,2,0,1,1,0), (0,4,1,0,0,1), (1,6), (0,3,1,0,1,0), (1,11),
    (0,5,0,1,0,0), (1,9), (0,3,1,0,1,1), (1,10), (0,2,7,0,1,0), (1,8), (0,4,7,0,0,1), (1,15), (0,5,1,1,0,0), (1,13),
    (0,0,6,0,1,1), (0,1,1,1,0,0), (0,2,6,0,1,1), (1,14), (0,3,2,0,0,0), (1,12), (0,4,0,2,1,0), (1,18), (0,5,7,1,1,1),
    (1,19), (0,2,6,0,0,0), (1,17), (0,3,2,0,0,1), (1,16), (0,4,0,2,0,1), (1,21), (0,5,7,1,1,0), (3,0,1,4,28), (1,22),
    (0,1,1,1,0,1), (0,0,7,1,1,0), (0,2,7,1,1,0), (1,23), (0,4,2,0,1,0), (1,20), (0,3,0,2,1,1), (1,27), (0,5,7,1,0,1),
    (0,2,7,1,0,1), (0,3,1,1,0,1), (0,4,0,2,1,1), (1,28), (0,0,1,2,0,0), (0,5,1,1,0,1), (1,33), (0,1,0,3,1,0),
    (0,2,0,3,1,0), (0,3,1,2,0,0), (0,4,1,2,0,0), (1,24), (1,25), (1,26), (1,31), (0,0,5,0,1,1), (1,36),
    (0,1,3,0,0,1), (1,37), (0,3,0,3,0,1), (1,34), (0,2,7,2,1,1), (0,4,7,2,1,1), (1,29), (1,30), (1,32), (1,40),
    (0,5,7,1,0,0), (1,35), (0,0,5,0,0,0), (0,1,3,0,0,0), (1,41), (0,2,6,1,1,0), (1,43), (0,3,1,2,1,1), (0,4,3,0,0,0),
    (0,5,6,1,1,0), (0,0,6,1,1,0), (1,46), (0,1,2,1,0,1), (0,2,5,0,1,1), (0,4,5,0,1,1), (0,3,0,3,1,0), (1,38), (1,39),
    (1,42), (1,45), (0,0,6,1,0,1), (0,5,6,1,0,1), (1,51), (0,1,7,3,1,0), (0,2,7,3,1,0), (0,4,3,0,0,1), (1,52),
    (0,3,2,2,0,0), (1,44), (1,47), (0,0,2,2,0,0), (3,2,8,24,29), (0,5,2,1,0,1), (1,56), (0,1,1,3,0,1), (0,3,1,3,0,1),
    (1,58), (0,2,7,3,1,1), (0,4,2,2,0,0), (1,48), (1,49), (1,50), (1,53), (0,5,2,2,0,0), (0,0,7,3,1,1), (1,62),
    (0,1,5,1,1,0), (1,55), (0,4,3,0,1,1), (1,63), (0,3,2,2,1,1), (0,2,5,1,1,0), (1,54), (1,57), (1,65),
    (0,0,6,2,1,0), (0,5,5,1,1,0), (1,68), (0,1,4,0,1,1), (0,4,2,2,1,1), (0,2,6,2,1,1), (0,3,3,0,0,0), (1,59), (1,60),
    (1,61), (1,64), (1,69), (0,0,5,1,1,1), (1,75), (0,5,3,1,0,1), (1,76), (0,1,3,2,0,0), (0,4,3,2,0,0), (1,74),
    (0,2,6,3,1,0), (0,3,3,2,0,0), (1,66), (1,67), (1,70), (0,0,6,3,1,0), (1,81), (0,1,6,3,1,1), (0,4,4,0,1,1),
    (0,2,6,3,1,1), (1,80), (0,3,2,3,0,1), (1,71), (1,72), (1,73), (1,85), (0,5,5,1,0,0), (1,82), (0,0,2,3,0,0),
    (1,88), (0,1,4,1,1,0), (1,87), (0,4,3,2,1,1), (0,2,6,2,0,1), (0,3,3,2,1,1), (1,77), (1,78), (1,79),
    (0,5,4,1,1,0), (3,3,5,6,12,20,30), (0,0,3,1,0,0), (1,94), (0,1,4,0,0,0), (1,91), (0,4,4,0,0,1), (1,83), (1,84),
    (1,86), (1,96), (0,3,3,2,0,1), (1,99), (0,2,5,3,1,0), (0,0,5,3,1,0), (1,98), (0,1,3,3,0,0), (1,100),
    (0,4,4,2,0,0), (1,89), (1,90), (1,92), (1,93), (1,105), (0,3,3,3,0,1), (1,104), (0,0,5,3,1,1), (0,2,5,3,1,1),
    (1,95), (1,97), (1,101), (1,102), (1,103), (1,106), (1,107), (1,108), (1,109), (1,110), (1,111), (1,112),
    (3,7,9,10,14,21,25,31), (1,113), (1,114), (1,115), (1,116), (1,117), (1,118), (1,119), (1,120), (1,121),
    (3,11,22,26,27), (1,122), (1,123), (3,13,15,16,17,18,19,23),
)


def arrives(way, piece):
    dy, pair, half, part = piece
    if way < 2:
        return (dy, pair, 1 - half, part)
    if way == 2:
        return ((dy - 1) % 8, pair, half, part)
    if way == 3:
        return ((dy + 1) % 8, pair, half, part)
    if way == 4:
        return (dy, (1, 0, 3, 2)[pair], half, part)
    return (dy, (0, 2, 1, 3)[pair], half, part)


def dot(a, b):
    return jnp.dot(a, b, preferred_element_type=jnp.float32)


def dot_general(a, b, ca, cb):
    return lax.dot_general(a, b, (((ca,), (cb,)), ((), ())), preferred_element_type=jnp.float32)


def kernel(
    x_hbm, t_hbm, rlen, scale_hbm, wq, wk, wv, wo, wd, aup_hbm,
    out_ref,
    xs, ts, scale, aup, nx, W, acc, kv, att, vgs, vgr, vgo, mgs, mgr,
    dkeep, dsend, drecv, s1, r1y, r1z, s2y, s2z, r2y, r2z, s3, r3, s4, r4,
    us, uxs, uxr, uys, uyr, uzs, uzr, ucs, ucr, uas, uer, stat,
    in_sem, ag_s, ag_r, cc_s, cc_r, kv_s, kv_r, vg_s, vg_r, mg_s, mg_r, dc_s, dc_r,
    y1_s, y1_r, z1_s, z1_r, y2_s, y2_r, z2_s, z2_r, x3_s, x3_r, c4_s, c4_r,
    uc_s, uc_r, ux_s, ux_r, uy_s, uy_r, uz_s, uz_r, ue_s, ue_r, ua_s, ua_r,
):
    f32, bf16 = jnp.float32, jnp.bfloat16
    dp, f, x = lax.axis_index("dp"), lax.axis_index("fsdp"), lax.axis_index("seq")
    h, y, zl, c = f // 8, f % 8, dp // 2, dp % 2
    z = h * 2 + zl

    def dev(xx, yy, zz, cc):
        return {"dp": (zz % 2) * 2 + cc, "fsdp": (zz // 2) * 8 + yy, "seq": xx}

    outer = (z + 7 + 2 * zl) % 8
    inner = (z + 1 + 6 * zl) % 8
    sib = dev(x, y, z, 1 - c)
    ways = [
        dev((x + 1) % 4, y, z, c),
        dev((x + 3) % 4, y, z, c),
        dev(x, (y + 1) % 8, z, c),
        dev(x, (y + 7) % 8, z, c),
        dev(x, y, outer, c),
        dev(x, y, inner, c),
    ]

    def remote(src, dst, ss, rs, to):
        return pltpu.make_async_remote_copy(src_ref=src, dst_ref=dst, send_sem=ss, recv_sem=rs, device_id=to)

    in_x = pltpu.make_async_copy(x_hbm, xs, in_sem.at[0])
    in_t = pltpu.make_async_copy(t_hbm, ts, in_sem.at[1])

    own_in = [
        pltpu.make_async_copy(w, W.at[f, pl.ds(k * 288, 256), :], in_sem.at[2 + k])
        for k, w in enumerate((wq, wk, wv, wo))
    ]
    own_in += [
        pltpu.make_async_copy(
            wd.at[pl.ds((k % 2) * 32, 32), pl.ds((k // 2) * 128, 128)],
            W.at[f, pl.ds(k * 288 + 256, 32), :],
            in_sem.at[6 + k],
        )
        for k in range(4)
    ]
    in_scale = pltpu.make_async_copy(scale_hbm, scale, in_sem.at[10])
    in_aup = pltpu.make_async_copy(aup_hbm, aup, in_sem.at[11])
    for cp in own_in + [in_scale, in_aup]:
        cp.start()
    in_x.start()
    in_t.start()
    kv[...] = jnp.zeros_like(kv)

    barrier = pltpu.get_barrier_semaphore()
    greet = [sib]
    greet += [dev((x + o) % 4, y, z, c) for o in (1, 2, 3)]
    greet += [dev(x, (y + o) % 8, z, c) for o in range(1, 8)]
    greet += [dev(x, y, (z + o) % 8, c) for o in range(1, 8)]
    other = z + 1 - 2 * zl
    greet += [dev(x, (y + o) % 8, other, c) for o in range(1, 8)]
    for to in greet:
        pl.semaphore_signal(barrier, inc=1, device_id=to)
    acc[...] = jnp.zeros_like(acc)
    for cp in own_in + [in_scale, in_aup]:
        cp.wait()
    pl.semaphore_wait(barrier, len(greet))


    pairs = [h, (h + 3 + 2 * zl) % 4, (h + 1 + 2 * (1 - zl) * 0 + 2 * zl) % 4, (h + 2) % 4]
    pairs[1] = (h + 3 + 2 * zl) % 4
    pairs[2] = (h + 1 + 2 * zl) % 4

    def region(piece):
        dy, pair, half, part = piece
        rows = (c * 2 + (half + x) % 2) * 288 + part * (288 // PARTS)
        return W.at[pairs[pair] * 8 + (y + dy) % 8, pl.ds(pl.multiple_of(rows, 16), 288 // PARTS), :]

    groups = [do[1:] for do in GATHER if do[0] == 3]
    group_of = {block: k for k, blocks in enumerate(groups) for block in blocks}
    sends, came = [], []
    for do in GATHER:
        if do[0] == 0:
            n = len(sends)
            a = region(do[2:])
            came.append(arrives(do[1], do[2:]))
            sends.append(remote(a, a, ag_s.at[0], ag_r.at[n], ways[do[1]]))

    def half_block(dy, pair, half):
        rows = (c * 2 + (half + x) % 2) * 288
        return W.at[pairs[pair] * 8 + (y + dy) % 8, pl.ds(pl.multiple_of(rows, 16), 288), :]

    def whole(blocks, sem):
        ref = W.at[pl.ds(0, blocks), pl.ds(0, 576), :]
        return pltpu.make_async_copy(ref, ref, sem)

    parts_in = {}

    def arrive(n):
        dy, pair, half, _ = came[n]
        sends[n].wait_recv()
        parts_in[dy, pair, half] = parts_in.get((dy, pair, half), 0) + 1
        if parts_in[dy, pair, half] == PARTS:
            a = half_block(dy, pair, half)
            remote(a, a, cc_s.at[0], cc_r.at[group_of[dy * 4 + pair]], sib).start()

    def norm_rows():
        in_x.wait()
        in_t.wait()
        width = 1024

        def sums(i, carry):
            xx, xt = carry
            cols = pl.ds(pl.multiple_of(i * width, width), width)
            a = xs[:, cols].astype(f32)
            b = ts[:, cols].astype(f32)
            return xx + jnp.sum(a * a, axis=1, keepdims=True), xt + jnp.sum(a * b, axis=1, keepdims=True)

        zero = jnp.zeros((128, 1), f32)
        xx, xt = lax.fori_loop(0, 8192 // width, sums, (zero, zero))
        stat[0] = jnp.broadcast_to(xx, (128, 128))
        stat[1] = jnp.broadcast_to(xt, (128, 128))
        inv = lax.rsqrt(xx / 8192.0 + eps_norm)

        def rows(i, carry):
            cols = pl.ds(pl.multiple_of(i * width, width), width)
            nx[:, cols] = (xs[:, cols].astype(f32) * inv * scale[:, cols]).astype(bf16)
            return carry

        lax.fori_loop(0, 8192 // width, rows, 0)
        lane = lax.broadcasted_iota(jnp.int32, (128, 128), 1)
        token = lax.broadcasted_iota(jnp.int32, (128, 128), 0)
        position = (x * 64 + token % 64).astype(f32)
        rate = jnp.exp((lane % 64).astype(f32) * (-2.0 / 128.0 * math.log(theta_base)))
        angle = position * rate
        stat[2] = jnp.cos(angle)
        sine = jnp.sin(angle)
        stat[3] = jnp.where(lane < 64, -sine, sine)

    def multiply(blocks):
        whole(len(blocks) - (0 in blocks), cc_r.at[group_of[blocks[0]]]).wait()

        def body(i, carry):
            g = jnp.int32(0)
            for k, block in enumerate(blocks):
                g += jnp.where(i == k, 1, 0) * (pairs[block % 4] * 8 + (y + block // 4) % 8)
            cols = pl.ds(pl.multiple_of(g * 256, 256), 256)
            a = nx[:, cols]
            qk = jnp.concatenate([W[g, 0:256, :], W[g, 288:544, :]], axis=1)
            down = jnp.concatenate(
                [jnp.concatenate([W[g, 288 * k + 256 : 288 * k + 288, :] for k in (k0, k0 + 1)], axis=0) for k0 in (0, 2)],
                axis=1,
            )
            both = dot(a, qk)
            acc[0] += both[:, 0:128]
            acc[1] += both[:, 128:256]
            acc[2] += dot(a, W[g, 576:832, :])
            acc[3, :, 0:64] += dot_general(a, down, 1, 1)
            return carry

        lax.fori_loop(0, len(blocks), body, 0, unroll=2)

    def multiply_out(g, carry):
        cols = pl.ds(pl.multiple_of(g * 256, 256), 256)
        out = W[g, 864:1120, :]
        acc[5] += dot(xs[:, cols], out)
        acc[6] += dot(ts[:, cols], out)
        acc[7] += dot_general(out, out, 0, 0)
        return carry

    n = 0
    for do in GATHER:
        if do[0] == 0:
            sends[n].start()
            n += 1
        elif do[0] == 1:
            arrive(do[1])
        elif do[0] == 2:
            norm_rows()
        else:
            multiply(do[1:])


    def rope(v):
        return (v * stat[2] + pltpu.roll(v, 64, 1) * stat[3]).astype(bf16)

    q = rope(acc[0])
    own = pl.ds(pl.multiple_of(x * 64, 64), 64)
    d_in = acc[3, :, 0:64].astype(bf16)
    base = acc[2]
    k_own = rope(acc[1])
    v_ref = base.astype(bf16)
    v_pol = (base + dot(d_in, aup[...])).astype(bf16)
    for b in range(2):
        kv[0, b, own, :] = k_own[b * 64 : b * 64 + 64]
        kv[1, b, own, :] = v_ref[b * 64 : b * 64 + 64]
        kv[2, b, own, :] = v_pol[b * 64 : b * 64 + 64]
    kv_own = kv.at[:, :, own, :]
    kvs = [remote(kv_own, kv_own, kv_s.at[o], kv_r.at[o], dev((x + o) % 4, y, z, c)) for o in range(4)]
    for o in (1, 2, 3):
        @pl.when(x + o < 4)
        def _():
            kvs[o].start()

    def waitkv():
        for o in (1, 2, 3):
            @pl.when(x + o < 4)
            def _():
                kvs[o].wait_send()

    def waitvg():
        for o in (1, 2, 3):
            @pl.when(x - o >= 0)
            def _():
                vgc[o].wait_send()

    lax.fori_loop(0, 32, multiply_out, 0, unroll=2)
    g_hi = acc[7].astype(bf16)
    g_lo = (acc[7] - g_hi.astype(f32)).astype(bf16)
    whole(31, ag_s.at[0]).wait()
    whole(31, cc_s.at[0]).wait()
    for o in (1, 2, 3):
        @pl.when(x - o >= 0)
        def _():
            kvs[o].wait_recv()


    row = lax.broadcasted_iota(jnp.int32, (64, 256), 0)
    col = lax.broadcasted_iota(jnp.int32, (64, 256), 1)
    allowed = col <= row + x * 64
    mixed = [[], []]
    for b in range(2):
        s = dot_general(q[b * 64 : b * 64 + 64], kv[0, b], 1, 1) / math.sqrt(128.0)
        s = jnp.where(allowed, s, -1e30)
        e = jnp.exp(s - jnp.max(s, axis=1, keepdims=True))
        e = jnp.where(allowed, e, 0.0)
        w = (e / jnp.sum(e, axis=1, keepdims=True)).astype(bf16)
        att[b] = w
        for m in range(2):
            mixed[m].append(dot(w, kv[1 + m, b]).astype(bf16))

    xx, xt, po, to = stat[0][:, 0:1], stat[1][:, 0:1], acc[5], acc[6]
    logits, invs, projs = [], [], []
    for m in range(2):
        mix = jnp.concatenate(mixed[m], axis=0)
        mg = dot(mix, g_hi) + dot(mix, g_lo)
        mixf = mix.astype(f32)
        sq = xx + jnp.sum(mixf * (2.0 * po + mg), axis=1, keepdims=True)
        inv = lax.rsqrt(sq / 8192.0 + eps_norm)
        logits.append(inv * (xt + jnp.sum(mixf * to, axis=1, keepdims=True)))
        invs.append(inv)
        projs.append(po + mg)
    token = lax.broadcasted_iota(jnp.int32, (128, 1), 0)
    start = jnp.where(token < 64, 256 - rlen[0], 256 - rlen[1])
    sign = jnp.where(token < 64, 1.0, -1.0)
    resp = jnp.where(x * 64 + token % 64 >= start, sign, 0.0)
    part = jnp.sum(resp * (logits[1] - logits[0]), axis=0, keepdims=True)

    mgs[...] = jnp.broadcast_to(part, (8, 128))
    mgc = [remote(mgs, mgr.at[o], mg_s.at[o], mg_r.at[o], dev((x + o) % 4, y, z, c)) for o in range(4)]
    for o in (1, 2, 3):
        mgc[o].start()

    head = (resp * invs[1] * (to - (logits[1] / 8192.0) * invs[1] * projs[1])).astype(bf16)
    for b in range(2):
        terms = dot_general(att[b], head[b * 64 : b * 64 + 64], 0, 0)
        vgs[b] = terms.astype(bf16)
        vgo[b] = terms
    vgc = []
    for o in range(4):
        target = (x + 4 - o) % 4
        src = vgs.at[:, pl.ds(pl.multiple_of(target * 64, 64), 64), :]
        vgc.append(remote(src, vgr.at[o], vg_s.at[o], vg_r.at[o], dev(target, y, z, c)))
    for o in (1, 2, 3):
        @pl.when(x - o >= 0)
        def _():
            vgc[o].start()
    for o in (1, 2, 3):
        mgc[o].wait()
    margin = beta_dpo * (mgs[...] + mgr[1] + mgr[2] + mgr[3])
    pull = (-beta_dpo / 128.0) / (1.0 + jnp.exp(margin))
    loss = jnp.maximum(-margin, 0.0) + jnp.log1p(jnp.exp(-jnp.abs(margin)))
    mine = [vgo[b, own, :] for b in range(2)]
    total = jnp.concatenate(mine, axis=0)
    vgo[0, 0:128, :] = total
    for o in (1, 2, 3):
        @pl.when(x + o < 4)
        def _():
            vgc[o].wait_recv()
            vgo[0, 0:128, :] += vgr[o].reshape(128, 128).astype(f32)
    vg = (vgo[0, 0:128, :] * pull[0:1, :]).astype(bf16)


    up = dot_general(d_in, vg, 0, 0)
    agt = dot_general(aup[...], vg, 1, 1).astype(bf16)

    us[...] = up
    keep = pl.ds(pl.multiple_of(c * 32, 32), 32)
    give = pl.ds(pl.multiple_of(32 - c * 32, 32), 32)
    ucs[32:40, :] = loss
    ucs[0:32, :] = us[give, :]
    uc = remote(ucs, ucr, uc_s.at[0], uc_r.at[0], sib)
    uc.start()

    ag_both = jnp.where(c == 0, jnp.concatenate([agt[32:64], agt[0:32]], axis=0), agt)
    dcs = []
    for n in range(4):
        for i in range(2):
            g = n * 8 + i * 4
            both = dot(ag_both, nx[:, g * 256 : g * 256 + 1024])
            for k in range(4):
                dsend[g + k] = both[0:32, k * 256 : k * 256 + 256].astype(bf16)
                dkeep[g + k] = both[32:64, k * 256 : k * 256 + 256]
        cp = remote(dsend.at[pl.ds(n * 8, 8)], drecv.at[pl.ds(n * 8, 8)], dc_s.at[n], dc_r.at[n], sib)
        cp.start()
        dcs.append(cp)

    uc.wait()
    uxs[...] = us[keep, :] + ucr[0:32, :]
    uys[8:16, :] = loss + ucr[32:40, :]
    uxc = []
    for o in range(4):
        tx = (x + o) % 4
        src = uxs.at[pl.ds(pl.multiple_of(tx * 8, 8), 8), :]
        uxc.append(remote(src, uxr.at[o], ux_s.at[o], ux_r.at[o], dev(tx, y, z, c)))
    for o in (1, 2, 3):
        uxc[o].start()

    for n in range(4):
        dcs[n].wait_recv()
        s1[n] = (dkeep[n * 8 : n * 8 + 8] + drecv[n * 8 : n * 8 + 8].astype(f32)).astype(bf16)


    y1, z1 = [], []
    for o in range(8):
        ty, tz = (y + o) % 8, (z + o) % 8
        y1.append(remote(s1.at[:, ty, pl.ds(0, 16), :], r1y.at[o], y1_s.at[o], y1_r.at[o], dev(x, ty, z, c)))
        z1.append(remote(s1.at[tz // 2, pl.ds((tz % 2) * 4, 4), pl.ds(16, 16), :], r1z.at[o], z1_s.at[o], z1_r.at[o],
                         dev(x, y, tz, c)))
    for o in (4, 3, 5, 2, 6, 1, 7):
        y1[o].start()
        z1[o].start()
    for o in (1, 2, 3):
        uxc[o].wait()
    eighth = pl.ds(pl.multiple_of(x * 8, 8), 8)
    uys[0:8, :] = uxs[eighth, :] + uxr[1] + uxr[2] + uxr[3]
    uyc = [remote(uys, uyr.at[o], uy_s.at[o], uy_r.at[o], dev(x, (y + o) % 8, z, c)) for o in range(8)]
    for o in range(1, 8):
        uyc[o].start()
    for o in range(1, 8):
        y1[o].wait()
        z1[o].wait()
    sy = s1[:, y, 0:16, :].astype(f32)
    sz = s1[h, pl.ds(zl * 4, 4), 16:32, :].astype(f32)
    for o in range(1, 8):
        sy += r1y[o].astype(f32)
        sz += r1z[o].astype(f32)
    s2y[...] = sy.astype(bf16)
    s2z[...] = sz.astype(bf16)


    y2 = []
    for o in range(8):
        tz = (z + o) % 8
        y2.append(remote(s2y.at[tz // 2], r2y.at[o], y2_s.at[o], y2_r.at[o], dev(x, y, tz, c)))
    for o in range(1, 8):
        y2[o].start()
    z2 = []
    for j in range(4):
        for zz in range(2):
            ty = zl * 4 + j
            z2.append((remote(s2z.at[j], r2z.at[y], z2_s.at[j * 2 + zz], z2_r.at[y], dev(x, ty, h * 2 + zz, c)),
                       jnp.logical_and(ty == y, zz == zl), j))
    for cp, me, j in z2:
        @pl.when(jnp.logical_not(me))
        def _():
            cp.start()
        @pl.when(me)
        def _():
            r2z[y] = s2z[j]
    for o in range(1, 8):
        uyc[o].wait()
    tot = uys[...]
    for o in range(1, 8):
        tot += uyr[o]
    uzs[...] = tot
    uzc = [remote(uzs, uzr.at[o], uz_s.at[o], uz_r.at[o], dev(x, y, (z + o) % 8, c)) for o in range(8)]
    for o in range(1, 8):
        uzc[o].start()
    for o in range(1, 8):
        y2[o].wait()
    for cp, me, j in z2:
        @pl.when(jnp.logical_not(me))
        def _():
            cp.wait_send()
    for s in range(8):
        @pl.when(jnp.logical_not(jnp.logical_and(s == y, y // 4 == zl)))
        def _():
            remote(s2z.at[0], r2z.at[s], z2_s.at[0], z2_r.at[s], sib).wait_recv()
    ty_ = s2y[h].astype(f32)
    tz_ = r2z[0].astype(f32)
    for o in range(1, 8):
        ty_ += r2y[o].astype(f32)
        tz_ += r2z[o].astype(f32)
    for k in range(2):
        s3[k, 0:16, :] = ty_[:, k * 128 : k * 128 + 128]
        s3[k, 16:32, :] = tz_[:, k * 128 : k * 128 + 128]


    x3 = []
    for o in range(4):
        tx = (x + o) % 4
        x3.append(remote(s3.at[tx // 2], r3.at[o], x3_s.at[o], x3_r.at[o], dev(tx, y, z, c)))
    for o in (1, 2, 3):
        x3[o].start()
    for o in range(1, 8):
        uzc[o].wait()
    tot = uzs[...]
    for o in range(1, 8):
        tot += uzr[o]
    uas[eighth, :] = tot[0:8, :]
    uac = []
    for o in range(4):
        ref = uas.at[eighth, :]
        uac.append(remote(ref, ref, ua_s.at[o], ua_r.at[o], dev((x + o) % 4, y, z, c)))
    for o in (1, 2, 3):
        uac[o].start()
    out_ref[128:136, :] = tot[8:16, :] * (1.0 / 128.0)
    for o in (1, 2, 3):
        x3[o].wait()
    mine = s3[x // 2] + r3[1] + r3[2] + r3[3]
    s4[...] = mine
    c4 = remote(s4, r4, c4_s.at[0], c4_r.at[0], sib)
    c4.start()
    for o in (1, 2, 3):
        uac[o].wait()
    ue = remote(uas, uer, ue_s.at[0], ue_r.at[0], sib)
    ue.start()
    out_ref[keep, :] = uas[...]
    for o in (1, 2, 3):
        @pl.when(x + o < 4)
        def _():
            kvs[o].wait_send()
        @pl.when(x - o >= 0)
        def _():
            vgc[o].wait_send()
    for n in range(4):
        dcs[n].wait_send()
    c4.wait()
    ue.wait()
    out_ref[give, :] = uer[...]
    low = jnp.where(c == 0, s4[...], r4[...])
    high = jnp.where(c == 0, r4[...], s4[...])
    whole = jnp.concatenate([low, high], axis=0)
    whole = jnp.where(x % 2 == 0, whole, pltpu.roll(whole, 64, 1))
    out_ref[64:128, 0:64] = whole.T[0:64, :]
    out_ref[64:128, 64:128] = jnp.zeros((64, 64), f32)


def split(packed, loss_ref, gdown_ref, gup_ref):
    loss_ref[0, 0] = jnp.max(packed[128:136, :])
    gdown_ref[...] = packed[64:128, 0:64]
    gup_ref[...] = packed[0:64, :]


def step(x_in, t_in, rlen, scale, wq, wk, wv, wo, wd, aup):
    f32, bf16 = jnp.float32, jnp.bfloat16
    V = pltpu.VMEM
    D = pltpu.SemaphoreType.DMA
    vm = pl.BlockSpec(memory_space=pltpu.VMEM)
    hb = pl.BlockSpec(memory_space=pl.ANY)
    packed = pl.pallas_call(
        kernel,
        name="dpo_step",
        out_shape=jax.ShapeDtypeStruct((136, 128), f32),
        in_specs=[hb, hb, pl.BlockSpec(memory_space=pltpu.SMEM)] + [hb] * 7,
        out_specs=vm,
        scratch_shapes=[
            V((128, 8192), bf16), V((128, 8192), bf16), V((1, 8192), f32), V((64, 128), bf16), V((128, 8192), bf16),
            V((32, 1152, 128), bf16), V((8, 128, 128), f32), V((3, 2, 256, 128), bf16), V((2, 64, 256), bf16),
            V((2, 256, 128), bf16), V((4, 2, 64, 128), bf16), V((2, 256, 128), f32), V((8, 128), f32), V((4, 8, 128), f32),
            V((32, 32, 256), f32), V((32, 32, 256), bf16), V((32, 32, 256), bf16), V((4, 8, 32, 256), bf16),
            V((8, 4, 16, 256), bf16), V((8, 4, 16, 256), bf16), V((4, 16, 256), bf16), V((4, 16, 256), bf16),
            V((8, 16, 256), bf16), V((8, 16, 256), bf16), V((2, 32, 128), f32), V((4, 32, 128), f32),
            V((32, 128), f32), V((32, 128), f32),
            V((64, 128), f32), V((32, 128), f32), V((4, 8, 128), f32), V((16, 128), f32), V((8, 16, 128), f32),
            V((16, 128), f32), V((8, 16, 128), f32), V((40, 128), f32), V((40, 128), f32), V((32, 128), f32), V((32, 128), f32),
            V((4, 128, 128), f32),
            D((12,)), D((1,)), D((SENDS,)), D((1,)), D((8,)), D((4,)), D((4,)), D((4,)), D((4,)), D((4,)), D((4,)),
            D((4,)), D((4,)), D((8,)), D((8,)), D((8,)), D((8,)), D((8,)), D((8,)), D((8,)), D((8,)), D((4,)), D((4,)),
            D((1,)), D((1,)), D((1,)), D((1,)), D((4,)), D((4,)), D((8,)), D((8,)), D((8,)), D((8,)), D((1,)), D((1,)), D((4,)), D((4,)),
        ],
        compiler_params=pltpu.CompilerParams(
            collective_id=0, has_side_effects=True, vmem_limit_bytes=56 * 2**20
        ),
    )(
        x_in.reshape(128, 8192), t_in.reshape(128, 8192), rlen, scale.reshape(1, 8192), wq, wk, wv, wo, wd.T, aup
    )
    loss, gdown, gup = pl.pallas_call(
        split,
        name="split",
        out_shape=(
            jax.ShapeDtypeStruct((1, 1), f32),
            jax.ShapeDtypeStruct((64, 64), f32),
            jax.ShapeDtypeStruct((64, 128), f32),
        ),
        in_specs=[vm],
        out_specs=(pl.BlockSpec(memory_space=pltpu.SMEM), vm, vm),
    )(packed)
    return loss.reshape(()), gdown, gup


def solution(mesh):
    return jax.shard_map(
        step,
        mesh=mesh,
        in_specs=(
            P(("dp", "fsdp"), "seq", None),
            P(("dp", "fsdp"), "seq", None),
            P(("dp", "fsdp")),
            P(),
            P("fsdp", None),
            P("fsdp", None),
            P("fsdp", None),
            P("fsdp", None),
            P("fsdp", None),
            P(),
        ),
        out_specs=(P(), P(("fsdp", "seq"), None), P()),
        check_vma=False,
    )
```
